128 devices in a mesh: track: 16 (over x, y_lo, core), cols: 8 (over y_hi, z).
Axes of the slice: x: 4, y: 4 (y_hi: 2, y_lo: 2; y = y_hi * 2 + y_lo), z: 4, core: 2. Of those that a mesh axis runs over, the one named last changes fastest.
Arguments:
- design: bfloat16 [8192, 4096], P('track', 'cols'), may hold values from -0.0625 to 0.0625
- seg_start: int32 [8192], P('track'), may hold values from 0 to 8191, as said below
- seg_table: int32 [8192], P('track'), may hold values from 0 to 7, as said below
- taps: bfloat16 [8, 97], replicated, may hold values from -1.25 to 1.25
- ridge: float32 [4096], replicated, may hold values from 0.3 to 3
- col_perm: int32 [4096], replicated, may hold values from 0 to 4095, each once
Outputs:
- normals: float32 [4096, 4096], P('track', 'cols')
- factor: float32 [4096, 1024], P('track', 'cols')
The draws below stay inside these ranges and needn't reach their ends.
Inputs may be any that keep to these rules, and one draw needn't show every extreme that they name: seg_start[r] is the first row of the run of consecutive rows that holds row r; it never exceeds r, row 0 starts a run, the last row starts a run of its own, and all rows of a run carry the same value. `seg_table`: all rows with the same seg_start carry the same table. `col_perm`: each of 0 to 4095 once.
All inputs are finite; a program needn't handle non-finite values.
Results may differ from the reference program's by a relative error of at most 0.0019.
Values may be sent and summed in bfloat16 or wider, within the bound.
No kernel may reach another device: no remote copies, remote signals or barrier semaphores. Data moves between devices by JAX's collectives and lax.ppermute only.
A program may use at most 64 MiB of HBM per device.

```python
import math
import jax
import jax.numpy as jnp
from jax import lax

SLAB = 4096
PANEL = 1024
TAPS = 97
TABLES = 8
ROW_DEV = 512
ROWS = 8192


def segment_layout(key):
    marks = jax.random.randint(jax.random.fold_in(key, 11), (ROWS,), 0, max(ROW_DEV // 8, 2))
    places = jnp.arange(ROWS, dtype=jnp.int32)
    begins = jnp.where((marks == 0) | (places == 0) | (places == ROWS - 1), places, 0)
    firsts = lax.cummax(begins)
    tables = jax.random.randint(jax.random.fold_in(key, 12), (ROWS,), 0, TABLES)
    return (firsts.astype(jnp.int32), jnp.take(tables, firsts).astype(jnp.int32))


def draw_seg_start(key, part):
    return segment_layout(key)[0]


def draw_seg_table(key, part):
    return segment_layout(key)[1]


def block_levels(stream_key, extent, cuts, smallest, high):
    def one(position, parts):
        steps = jax.random.uniform(jax.random.fold_in(jax.random.fold_in(stream_key, 6), position), (parts,), jnp.float32, smallest / len(cuts), high / len(cuts))
        return jnp.repeat(jnp.exp(steps), extent[position] // parts).reshape((-1,) + (1,) * (len(extent) - position - 1))

    factor_of = one(*cuts[0])
    for cut in cuts[1:]:
        factor_of = factor_of * one(*cut)
    return factor_of


def centred(rng, dims, scale, bound, cuts=(), kind=jnp.bfloat16):
    result = scale * jax.random.normal(rng, dims, jnp.float32)
    if cuts:
        result = result * block_levels(rng, dims, cuts, -0.22, 0.18)
    return jnp.clip(result, -bound, bound).astype(kind)


def setup_inputs(seed: int = 0) -> dict:
    splits = jax.random.split(jax.random.key(seed), 7)
    design = centred(splits[0], (ROWS, SLAB), ROWS ** -0.5, 0.0625, ((0, 16), (1, 8)))
    seg_start = draw_seg_start(jax.random.fold_in(splits[6], 71), 0)
    seg_table = draw_seg_table(jax.random.fold_in(splits[6], 71), 0)
    taps = centred(splits[3], (TABLES, TAPS), (TAPS // 4) ** -0.5, 1.25)
    ridge = jnp.clip(jnp.exp(jax.random.uniform(splits[4], (SLAB,), jnp.float32, math.log(0.3), math.log(3.0))), 0.3, 3.0)
    col_perm = jax.random.permutation(splits[5], SLAB).astype(jnp.int32)
    return dict(design=design, seg_start=seg_start, seg_table=seg_table, taps=taps, ridge=ridge, col_perm=col_perm)


def filter_rows(local, ext_top, seg_start, seg_table, taps, first_row):
    halo_rows = taps.shape[1] - 1
    row_count, columns = local.shape
    block = min(512, row_count)
    blocks = row_count // block
    extended = jnp.concatenate([ext_top, local], axis=0)
    upper = extended[:row_count].reshape(blocks, block, columns)
    lower_part = local.reshape(blocks, block, columns)[:, block - halo_rows:, :]
    windows = jnp.concatenate([upper, lower_part], axis=1)
    onehot = (seg_table[:, None] == jnp.arange(taps.shape[0], dtype=jnp.int32)[None, :]).astype(jnp.float32)
    row_taps = jnp.dot(onehot, taps.astype(jnp.float32), precision=lax.Precision.HIGHEST)
    flipped = row_taps[:, ::-1].reshape(blocks, block, halo_rows + 1)
    span = block + halo_rows
    padded = jnp.pad(flipped, ((0, 0), (0, 0), (0, span - halo_rows)))
    skewed = padded.reshape(blocks, block * (span + 1))[:, :block * span].reshape(blocks, block, span)
    offsets = (jnp.arange(blocks, dtype=jnp.int32) * block)[:, None, None]
    col_rows = first_row + offsets - halo_rows + jnp.arange(span, dtype=jnp.int32)[None, None, :]
    starts = seg_start.reshape(blocks, block)[:, :, None]
    coefs = jnp.where(col_rows >= starts, skewed, 0.0)
    summed = jnp.einsum('brj,bjc->brc', coefs, windows.astype(jnp.float32), precision=lax.Precision.HIGHEST)
    return summed.reshape(row_count, columns).astype(jnp.bfloat16)

def reference(design, seg_start, seg_table, taps, ridge, col_perm):
    ext_top = jnp.zeros((taps.shape[1] - 1, design.shape[1]), jnp.bfloat16)
    filtered = filter_rows(design, ext_top, seg_start, seg_table, taps, 0)
    normals = jnp.dot(filtered.T.astype(jnp.float32), filtered.astype(jnp.float32), preferred_element_type=jnp.float32) + jnp.diag(ridge)
    panel_ids = col_perm[:PANEL]
    panel_cols = jnp.take(normals, panel_ids, axis=1)
    panel_block = jnp.take(panel_cols, panel_ids, axis=0)
    lower = jnp.linalg.cholesky(panel_block)
    factor = lax.linalg.triangular_solve(lower, panel_cols, left_side=False, lower=True, transpose_a=True)
    return (normals, factor)
```

```python
import functools

import jax
import jax.numpy as jnp
from jax import lax
from jax.experimental import pallas as pl
from jax.experimental.pallas import tpu as pltpu
from jax.sharding import PartitionSpec as P

PANEL = 1024
NB = 128
SUB = 8
ROWS_T = (((0,), (0,)), ((), ()))
HIGH = lax.Precision.HIGHEST


def dot_f32(a, b, dims=(((1,), (0,)), ((), ()))):
    return lax.dot_general(a, b, dims, precision=HIGH, preferred_element_type=jnp.float32)


def gather(x, axis):
    copies = jnp.broadcast_to(x[None], (lax.axis_size(axis),) + x.shape)
    return lax.all_to_all(copies, axis, 0, 0)


def filter_kernel(first_ref, halo_ref, local_ref, start_ref, table_ref, taps_ref, out_ref, ext_ref):
    halo_rows = halo_ref.shape[0]
    row_count, columns = local_ref.shape
    ext_ref[:halo_rows] = halo_ref[...]
    ext_ref[halo_rows : halo_rows + row_count] = local_ref[...]
    ext_ref[halo_rows + row_count :] = jnp.zeros_like(ext_ref[halo_rows + row_count :])
    span = 2 * NB
    taps = taps_ref[...]
    tables = taps.shape[0]
    lane = lax.broadcasted_iota(jnp.int32, (NB, span), 1)
    for b in range(row_count // NB):
        rows = pl.ds(b * NB, NB)
        choice = lax.broadcasted_iota(jnp.int32, (NB, tables), 1) == table_ref[rows, :]
        row_taps = jnp.dot(
            choice.astype(jnp.float32).astype(jnp.bfloat16), taps, preferred_element_type=jnp.float32
        )
        skewed = pltpu.roll(row_taps, 0, 1, stride=1, stride_axis=0)
        source = first_ref[0] + b * NB - halo_rows + lane
        coefs = jnp.where(source >= start_ref[rows, :], skewed, 0.0).astype(jnp.bfloat16)
        window = ext_ref[pl.ds(b * NB, span), :]
        out_ref[rows, :] = jnp.dot(coefs, window, preferred_element_type=jnp.float32).astype(
            jnp.bfloat16
        )


def filter_rows(local, ext_top, seg_start, seg_table, taps, first_row):
    row_count, columns = local.shape
    halo_rows = ext_top.shape[0]
    flipped = jnp.pad(taps[:, ::-1], ((0, 0), (0, 2 * NB - taps.shape[1])))
    vmem = pl.BlockSpec(memory_space=pltpu.VMEM)
    return pl.pallas_call(
        filter_kernel,
        out_shape=jax.ShapeDtypeStruct(local.shape, jnp.bfloat16),
        in_specs=[pl.BlockSpec(memory_space=pltpu.SMEM)] + [vmem] * 5,
        out_specs=vmem,
        scratch_shapes=[pltpu.VMEM((row_count + NB, columns), jnp.bfloat16)],
        compiler_params=pltpu.CompilerParams(vmem_limit_bytes=16 * 2**20),
    )(
        first_row.reshape(1),
        ext_top,
        local,
        seg_start[:, None],
        seg_table[:, None],
        flipped,
    )


def factor_groups(groups):
    groups = list(groups)
    shape = (SUB, NB)
    lane = lax.broadcasted_iota(jnp.int32, shape, 1)
    sub = lax.broadcasted_iota(jnp.int32, shape, 0)
    for s in range(len(groups)):
        top = groups[s]
        base = s * SUB
        rows = [jnp.broadcast_to(top[i : i + 1, :], shape) for i in range(SUB)]
        t = {}
        for i in range(SUB):
            for j in range(i + 1):
                t[i, j] = jnp.broadcast_to(rows[i][:, base + j : base + j + 1], shape)
        inside = (lane >= base) & (lane < base + SUB)
        r, l, done = [], {}, []
        for k in range(SUB):
            r.append(lax.rsqrt(t[k, k]))
            for i in range(k + 1, SUB):
                l[i, k] = t[i, k] * r[k]
            for j in range(k + 1, SUB):
                for i in range(j, SUB):
                    t[i, j] = t[i, j] - l[i, k] * l[j, k]
        for i in range(SUB):
            acc = jnp.where(inside, (lane == base + i).astype(jnp.float32), rows[i])
            for j in range(i):
                acc = acc - l[i, j] * done[j]
            done.append(acc * r[i])
        packed = done[0]
        for i in range(1, SUB):
            packed = jnp.where(sub == i, done[i], packed)
        groups[s] = packed
        back = [None] * SUB
        for j in reversed(range(SUB)):
            acc = done[j]
            for i in range(j + 1, SUB):
                acc = acc - l[i, j] * back[i]
            back[j] = acc * r[j]
        for g in range(s + 1, len(groups)):
            acc = jnp.where(inside, 0.0, groups[g])
            for j in range(SUB):
                column = groups[g][:, base + j : base + j + 1]
                acc = acc - jnp.broadcast_to(column, shape) * back[j]
            groups[g] = acc
    return groups


def inverse_kernel(turn_ref, pieces_ref, out_ref, work_ref):
    size = work_ref.shape[0]
    blocks = size // NB
    row_piece = pieces_ref.shape[1]
    for i in range(size // row_piece):
        for j in range(blocks):
            work_ref[i * row_piece : (i + 1) * row_piece, j * NB : (j + 1) * NB] = pieces_ref[
                i * blocks + j
            ]
    triangle = lax.broadcasted_iota(jnp.int32, (NB, NB), 0) >= lax.broadcasted_iota(
        jnp.int32, (NB, NB), 1
    )

    def step(m, _):
        here = pl.ds(pl.multiple_of(m * NB, NB), NB)
        start = pl.multiple_of(m * NB, NB)
        groups = [work_ref[pl.ds(start + SUB * g, SUB), here] for g in range(NB // SUB)]
        inverse = jnp.where(triangle, jnp.concatenate(factor_groups(groups), axis=0), 0.0)
        work_ref[here, :] = dot_f32(inverse, work_ref[here, :])
        work_ref[here, here] = inverse
        again = dot_f32(inverse, work_ref[here, :], ROWS_T)

        def lower(i, _):
            below = pl.ds(pl.multiple_of(i * NB, NB), NB)
            left = work_ref[below, here]
            work_ref[below, here] = jnp.zeros((NB, NB), jnp.float32)
            work_ref[below, :] -= dot_f32(left, again)
            return 0

        lax.fori_loop(m + 1, blocks, lower, 0)
        return 0

    lax.fori_loop(0, blocks, step, 0)
    turn = turn_ref[0]
    row = lax.broadcasted_iota(jnp.int32, out_ref.shape, 0) + turn * NB
    col = lax.broadcasted_iota(jnp.int32, out_ref.shape, 1)
    mine = work_ref[pl.ds(pl.multiple_of(turn * NB, NB), NB), :]
    out_ref[...] = jnp.where(row >= col, mine, 0.0)


def inverse_rows(pieces, turn):
    vmem = pl.BlockSpec(memory_space=pltpu.VMEM)
    return pl.pallas_call(
        inverse_kernel,
        out_shape=jax.ShapeDtypeStruct((NB, PANEL), jnp.float32),
        in_specs=[pl.BlockSpec(memory_space=pltpu.SMEM), vmem],
        out_specs=vmem,
        scratch_shapes=[pltpu.VMEM((PANEL, PANEL), jnp.float32)],
        compiler_params=pltpu.CompilerParams(vmem_limit_bytes=40 * 2**20),
    )(turn.reshape(1), pieces)


def body(design, seg_start, seg_table, taps, ridge, col_perm):
    row_count, width = design.shape
    halo_rows = taps.shape[1] - 1
    track, cols = lax.axis_size("track"), lax.axis_size("cols")
    t, c = lax.axis_index("track"), lax.axis_index("cols")
    panel_blk = PANEL // cols
    panel_piece = PANEL // track
    slab = width * cols
    row_blk = slab // track
    panel_ids = col_perm[:PANEL]

    pairs = [(i, i + 1) for i in range(track - 1)]
    ext_top = lax.ppermute(design[row_count - halo_rows :], "track", pairs)
    filtered = filter_rows(design, ext_top, seg_start, seg_table, taps, t * row_count)
    gathered = gather(filtered, "cols")

    places = jnp.arange(slab, dtype=jnp.int32).reshape(cols, width)
    chosen = (places[:, :, None] == panel_ids[None, None, :]).astype(jnp.bfloat16)
    panel = lax.dot_general(
        gathered, chosen, (((0, 2), (0, 1)), ((), ())), preferred_element_type=jnp.float32
    ).astype(jnp.bfloat16)
    panel_mine = lax.dynamic_slice_in_dim(panel, c * panel_blk, panel_blk, 1)
    block_part = lax.dot_general(panel, panel_mine, ROWS_T, preferred_element_type=jnp.float32)
    block_parts = lax.all_to_all(block_part.reshape(track, panel_piece, panel_blk), "track", 0, 0)
    block_piece = jnp.sum(block_parts, axis=0)
    prow = t * panel_piece + jnp.arange(panel_piece, dtype=jnp.int32)
    pcol = c * panel_blk + jnp.arange(panel_blk, dtype=jnp.int32)
    mine_ids = lax.dynamic_slice_in_dim(panel_ids, c * panel_blk, panel_blk)
    mine_ridge = jnp.take(ridge, mine_ids)
    block_piece += jnp.where(prow[:, None] == pcol[None, :], mine_ridge[None, :], 0.0)
    pieces = gather(block_piece, ("track", "cols"))
    inverse = inverse_rows(pieces, c)

    contract = (((1,), (0,)), ((), ()))
    part = lax.dot_general(gathered, filtered, contract, preferred_element_type=jnp.float32)
    part_cols = lax.dot_general(gathered, panel_mine, contract, preferred_element_type=jnp.float32)
    own_cols = lax.psum_scatter(
        part_cols.reshape(slab, panel_blk), "track", scatter_dimension=0, tiled=True
    )
    row_ids = t * row_blk + jnp.arange(row_blk, dtype=jnp.int32)
    col_ids = c * width + jnp.arange(width, dtype=jnp.int32)
    own_cols += jnp.where(row_ids[:, None] == mine_ids[None, :], mine_ridge[None, :], 0.0)
    panel_rows = gather(own_cols, "cols")
    sums = lax.psum_scatter(part.reshape(slab, width), "track", scatter_dimension=0, tiled=True)
    row_ridge = lax.dynamic_slice_in_dim(ridge, t * row_blk, row_blk)
    normals = sums + jnp.where(row_ids[:, None] == col_ids[None, :], row_ridge[:, None], 0.0)

    factor = lax.dot_general(
        panel_rows,
        inverse.reshape(panel_blk, cols, panel_blk),
        (((0, 2), (1, 2)), ((), ())),
        precision=HIGH,
        preferred_element_type=jnp.float32,
    )
    return (normals, factor)


def solution(mesh):
    in_specs = (P("track", "cols"), P("track"), P("track"), P(), P(), P())
    out_specs = (P("track", "cols"), P("track", "cols"))
    return jax.shard_map(body, mesh=mesh, in_specs=in_specs, out_specs=out_specs, check_vma=False)
```

```python
import jax
import jax.numpy as jnp
from jax import lax
from jax.experimental import pallas as pl
from jax.experimental.pallas import tpu as pltpu
from jax.sharding import Mesh
from jax.sharding import PartitionSpec as P

PANEL = 1024
NB = 128
HALF = 64
SUB = 8
BLOCKS = PANEL // NB
LIST = 9
SLICES = 5
NN = (((1,), (0,)), ((), ()))
NT = (((1,), (1,)), ((), ()))
HIGH = lax.Precision.HIGHEST
SPLIT = {"x": 4, "yl": 2, "core": 2, "yh": 2, "z": 4}
TRACK = ("x", "yl", "core")
COLS = ("yh", "z")
PAIRS = ("x", "yl")
CHIPS = ("x", "yl", "yh", "z")
SWAP = [(0, 1), (1, 0)]
VMEM = pl.BlockSpec(memory_space=pltpu.VMEM)
SMEM = pl.BlockSpec(memory_space=pltpu.SMEM)


def gather(x, axis):
    copies = jnp.broadcast_to(x[None], (lax.axis_size(axis),) + x.shape)
    return lax.all_to_all(copies, axis, 0, 0)


def scatter_sum(x, axis):
    size = lax.axis_size(axis)
    here = lax.axis_index(axis)
    total = lax.dynamic_index_in_dim(x, here, 0, keepdims=False)
    for step in range(1, size):
        pairs = [(i, i ^ step) for i in range(size)]
        sent = lax.dynamic_index_in_dim(x, here ^ step, 0, keepdims=False)
        total += lax.ppermute(sent, axis, pairs)
    return total


def filter_kernel(first_ref, halo_ref, local_ref, start_ref, table_ref, taps_ref, out_ref, ext_ref):
    halo_rows = halo_ref.shape[0]
    row_count, columns = local_ref.shape
    ext_ref[:halo_rows] = halo_ref[...]
    ext_ref[halo_rows : halo_rows + row_count] = local_ref[...]
    ext_ref[halo_rows + row_count :] = jnp.zeros_like(ext_ref[halo_rows + row_count :])
    span = 2 * NB
    taps = taps_ref[...]
    tables = taps.shape[0]
    lane = lax.broadcasted_iota(jnp.int32, (NB, span), 1)
    for b in range(row_count // NB):
        rows = slice(b * NB, (b + 1) * NB)
        choice = lax.broadcasted_iota(jnp.int32, (NB, tables), 1) == table_ref[rows, :]
        row_taps = jnp.dot(
            choice.astype(jnp.float32).astype(jnp.bfloat16), taps, preferred_element_type=jnp.float32
        )
        skewed = pltpu.roll(row_taps, 0, 1, stride=1, stride_axis=0)
        source = first_ref[0] + b * NB - halo_rows + lane
        coefs = jnp.where(source >= start_ref[rows, :], skewed, 0.0).astype(jnp.bfloat16)
        window = ext_ref[b * NB : b * NB + span, :]
        summed = jnp.dot(coefs, window, preferred_element_type=jnp.float32)
        out_ref[:, rows] = summed.T.astype(jnp.bfloat16)


def filter_rows(local, ext_top, seg_start, seg_table, taps, first_row):
    row_count, columns = local.shape
    flipped = jnp.pad(taps[:, ::-1], ((0, 0), (0, 2 * NB - taps.shape[1])))
    return pl.pallas_call(
        filter_kernel,
        out_shape=jax.ShapeDtypeStruct((columns, row_count), jnp.bfloat16),
        in_specs=[SMEM] + [VMEM] * 5,
        out_specs=VMEM,
        scratch_shapes=[pltpu.VMEM((row_count + NB, columns), jnp.bfloat16)],
        compiler_params=pltpu.CompilerParams(vmem_limit_bytes=16 * 2**20),
    )(
        first_row.reshape(1),
        ext_top,
        local,
        seg_start[:, None],
        seg_table[:, None],
        flipped,
    )


def listed(c, h):
    own = (c < BLOCKS // 2) | (h < 2 * (BLOCKS - c))
    if isinstance(c, int):
        return (2 * c + h, c) if own else (7 + h, BLOCKS - 1 - c)
    return jnp.where(own, 2 * c + h, 7 + h), jnp.where(own, c, BLOCKS - 1 - c)


def panel_kernel(turn_ref, ids_ref, slab_ref, out_ref, mine_ref, panel_ref):
    cols, width, rows = slab_ref.shape
    part = 2 * NB
    lane = lax.broadcasted_iota(jnp.int32, (part, width), 1)
    for p in range(PANEL // part):
        ids = ids_ref[p * part : (p + 1) * part, :]
        acc = jnp.zeros((part, rows), jnp.float32)
        for k in range(cols):
            chosen = (lane == ids - k * width).astype(jnp.float32).astype(jnp.bfloat16)
            acc += jnp.dot(chosen, slab_ref[k], preferred_element_type=jnp.float32)
        panel_ref[p * part : (p + 1) * part, :] = acc.astype(jnp.bfloat16)
    turn = turn_ref[0]
    mine_ref[...] = panel_ref[pl.ds(pl.multiple_of(turn * NB, NB), NB), :]
    for h in range(LIST):
        i, j = listed(turn, h)
        left = panel_ref[pl.ds(pl.multiple_of(i * HALF, HALF), HALF), :]
        right = panel_ref[pl.ds(pl.multiple_of(j * NB, NB), NB), :]
        out_ref[h * HALF : (h + 1) * HALF, :] = lax.dot_general(
            left, right, NT, preferred_element_type=jnp.float32
        )
    out_ref[LIST * HALF :, :] = jnp.zeros_like(out_ref[LIST * HALF :, :])


def panel_parts(turn, panel_ids, slab, track):
    rows = slab.shape[-1]
    return pl.pallas_call(
        panel_kernel,
        out_shape=(
            jax.ShapeDtypeStruct((track * SLICES * SUB, NB), jnp.float32),
            jax.ShapeDtypeStruct((NB, rows), jnp.bfloat16),
        ),
        in_specs=[SMEM, VMEM, VMEM],
        out_specs=(VMEM, VMEM),
        scratch_shapes=[pltpu.VMEM((PANEL, rows), jnp.bfloat16)],
        compiler_params=pltpu.CompilerParams(vmem_limit_bytes=40 * 2**20),
    )(turn.reshape(1), panel_ids[:, None], slab)


def halves(a):
    high = a.astype(jnp.bfloat16)
    return high, (a - high.astype(jnp.float32)).astype(jnp.bfloat16)


def product(a, b, dims=NN):
    (ah, al), (bh, bl) = halves(a), halves(b)

    def dot(u, v):
        return lax.dot_general(u, v, dims, preferred_element_type=jnp.float32)

    return dot(ah, bh) + (dot(ah, bl) + dot(al, bh))


def factor_groups(groups, tasks):
    groups = list(groups)
    count = len(groups)
    shape = (SUB, NB)
    lane = lax.broadcasted_iota(jnp.int32, shape, 1)
    sub = lax.broadcasted_iota(jnp.int32, shape, 0)
    share = -(-len(tasks) // count)
    for s in range(count):
        top = groups[s]
        base = s * SUB
        more = s + 1 < count

        def column(g, j):
            return jnp.broadcast_to(groups[g][:, base + j : base + j + 1], shape)

        rows = [jnp.broadcast_to(top[i : i + 1, :], shape) for i in range(SUB)]
        t = {}
        for i in range(SUB):
            for j in range(i + 1):
                t[i, j] = jnp.broadcast_to(rows[i][:, base + j : base + j + 1], shape)
        inside = (lane >= base) & (lane < base + SUB)
        for i in range(SUB):
            rows[i] = jnp.where(inside, (lane == base + i).astype(jnp.float32), rows[i])
        r, u = [], {}
        if more:
            below = [column(s + 1, j) for j in range(SUB)]
            following = jnp.where(inside, 0.0, groups[s + 1])
        for k in range(SUB):
            r.append(1.0 / t[k, k])
            for i in range(k + 1, SUB):
                u[i, k] = t[i, k] * r[k]
            for j in range(k + 1, SUB):
                t[j, j] = t[j, j] - (t[j, k] * t[j, k]) * r[k]
                for i in range(j + 1, SUB):
                    t[i, j] = t[i, j] - u[i, k] * t[j, k]
            for i in range(k + 1, SUB):
                rows[i] = rows[i] - u[i, k] * rows[k]
                if more:
                    below[i] = below[i] - u[i, k] * below[k]
            if more:
                following = following - (below[k] * r[k]) * rows[k]
        packed = rows[0] * lax.rsqrt(t[0, 0])
        for i in range(1, SUB):
            packed = jnp.where(sub == i, rows[i] * lax.rsqrt(t[i, i]), packed)
        groups[s] = packed
        if more:
            groups[s + 1] = following
        if s + 2 < count:
            back = [None] * SUB
            for j in reversed(range(SUB)):
                acc = rows[j] * r[j]
                for i in range(j + 1, SUB):
                    acc = acc - u[i, j] * back[i]
                back[j] = acc
            for g in range(s + 2, count):
                acc = jnp.where(inside, 0.0, groups[g])
                for j in reversed(range(SUB)):
                    acc = acc - column(g, j) * back[j]
                groups[g] = acc
        for task in tasks[s * share : (s + 1) * share]:
            task()
    return groups


def block(i):
    return slice(i * NB, (i + 1) * NB)


def place_pieces(side, ours_ref, theirs_ref, ridge_ref, work_ref):
    chips = ours_ref.shape[0]
    cols = BLOCKS
    for place in range(chips):
        pair, c = divmod(place, cols)
        for core in range(2):
            t = 2 * pair + core
            for e in range(SLICES):
                h, row = divmod(SLICES * t + e, HALF // SUB)
                if h >= LIST:
                    continue
                i, j = listed(c, h)
                here = slice(e * SUB, (e + 1) * SUB)
                value = jnp.where(
                    side == core, ours_ref[place, here, :], theirs_ref[place, here, :]
                )
                first = i * HALF + row * SUB
                work_ref[first : first + SUB, block(j)] = value
    eye = lax.broadcasted_iota(jnp.int32, (NB, NB), 0) == lax.broadcasted_iota(
        jnp.int32, (NB, NB), 1
    )
    for m in range(BLOCKS):
        work_ref[block(m), block(m)] += jnp.where(eye, ridge_ref[:, block(m)], 0.0)


def inverse_kernel(place_ref, ours_ref, theirs_ref, ridge_ref, out_ref, work_ref):
    place_pieces(place_ref[1], ours_ref, theirs_ref, ridge_ref, work_ref)
    triangle = lax.broadcasted_iota(jnp.int32, (NB, NB), 0) >= lax.broadcasted_iota(
        jnp.int32, (NB, NB), 1
    )
    tasks = []
    for m in range(BLOCKS):
        groups = [
            work_ref[m * NB + SUB * g : m * NB + SUB * (g + 1), block(m)] for g in range(NB // SUB)
        ]
        groups = factor_groups(groups, tasks)
        inverse = jnp.where(triangle, jnp.concatenate(groups, axis=0), 0.0)
        tasks = []
        left = {}
        if m + 1 < BLOCKS:
            left[m + 1] = product(work_ref[block(m + 1), block(m)], inverse, NT)
            work_ref[block(m + 1), block(m + 1)] -= product(left[m + 1], left[m + 1], NT)

        def finish(m=m, inverse=inverse):
            if m:
                work_ref[block(m), : m * NB] = product(inverse, work_ref[block(m), : m * NB])
            work_ref[block(m), block(m)] = inverse

        def solve(i, m=m, inverse=inverse, left=left):
            left[i] = product(work_ref[block(i), block(m)], inverse, NT)

        def spread(i, m=m, left=left):
            if m:
                work_ref[block(i), : m * NB] -= product(left[i], work_ref[block(m), : m * NB])
            work_ref[block(i), block(m)] = -product(left[i], work_ref[block(m), block(m)])

        def update(i, j, left=left):
            work_ref[block(i), block(j)] -= product(left[i], left[j], NT)

        tasks.append(finish)
        for i in range(m + 1, BLOCKS):
            if i > m + 1:
                tasks.append(lambda i=i, solve=solve: solve(i))
            tasks.append(lambda i=i, spread=spread: spread(i))
            for j in range(m + 1, i + 1):
                if i > m + 1:
                    tasks.append(lambda i=i, j=j, update=update: update(i, j))
    for task in tasks:
        task()
    turn = place_ref[0]
    row = lax.broadcasted_iota(jnp.int32, out_ref.shape, 0) + turn * NB
    col = lax.broadcasted_iota(jnp.int32, out_ref.shape, 1)
    mine = work_ref[pl.ds(pl.multiple_of(turn * NB, NB), NB), :]
    out_ref[...] = jnp.where(row >= col, mine, 0.0)


def inverse_rows(place, ours, theirs, panel_ridge):
    return pl.pallas_call(
        inverse_kernel,
        out_shape=jax.ShapeDtypeStruct((NB, PANEL), jnp.float32),
        in_specs=[SMEM, VMEM, VMEM, VMEM],
        out_specs=VMEM,
        scratch_shapes=[pltpu.VMEM((PANEL, PANEL), jnp.float32)],
        compiler_params=pltpu.CompilerParams(vmem_limit_bytes=40 * 2**20),
    )(place, ours, theirs, panel_ridge[None, :])


def body(design, seg_start, seg_table, taps, ridge, col_perm):
    row_count, width = design.shape
    halo_rows = taps.shape[1] - 1
    track, cols = lax.axis_size(TRACK), lax.axis_size(COLS)
    t, c, core = lax.axis_index(TRACK), lax.axis_index(COLS), lax.axis_index("core")
    slab = width * cols
    row_blk = slab // track
    panel_ids = col_perm[:PANEL]
    panel_ridge = jnp.take(ridge, panel_ids)

    pairs = [(i, i + 1) for i in range(track - 1)]
    ext_top = lax.ppermute(design[row_count - halo_rows :], TRACK, pairs)
    filtered = filter_rows(design, ext_top, seg_start, seg_table, taps, t * row_count)
    gathered = gather(filtered, COLS)

    block_part, panel_mine = panel_parts(c, panel_ids, gathered, track)
    block_parts = lax.all_to_all(block_part.reshape(track, SLICES * SUB, NB), TRACK, 0, 0)
    ours = gather(jnp.sum(block_parts, axis=0), CHIPS)

    slab_rows = gathered.reshape(track // 2, 2, row_blk, row_count)
    right = jnp.concatenate([filtered, panel_mine], axis=0)

    def rows_of(side):
        rows = lax.dynamic_index_in_dim(slab_rows, side, 1, keepdims=False)
        return lax.dot_general(
            rows, right, (((2,), (1,)), ((), ())), preferred_element_type=jnp.float32
        )

    sums = rows_of(core) + lax.ppermute(rows_of(1 - core), "core", SWAP)
    col_sums = scatter_sum(sums[:, :, width:], PAIRS)
    row_ids = t * row_blk + jnp.arange(row_blk, dtype=jnp.int32)
    mine_ids = lax.dynamic_slice_in_dim(panel_ids, c * NB, NB)
    mine_ridge = lax.dynamic_slice_in_dim(panel_ridge, c * NB, NB)
    own_cols = col_sums + jnp.where(
        row_ids[:, None] == mine_ids[None, :], mine_ridge[None, :], 0.0
    )
    narrow = sums[:, :, :width].astype(jnp.float16)
    narrow, own_cols, ours = lax.optimization_barrier((narrow, own_cols, ours))
    theirs = lax.ppermute(ours, "core", SWAP)
    parts = lax.all_to_all(narrow, PAIRS, 0, 0)
    panel_rows = lax.all_gather(own_cols, COLS)
    inverse = inverse_rows(jnp.stack([c, core]), ours, theirs, panel_ridge)
    col_ids = c * width + jnp.arange(width, dtype=jnp.int32)
    row_ridge = lax.dynamic_slice_in_dim(ridge, t * row_blk, row_blk)
    normals = jnp.sum(parts.astype(jnp.float32), axis=0) + jnp.where(
        row_ids[:, None] == col_ids[None, :], row_ridge[:, None], 0.0
    )
    factor = lax.dot_general(
        panel_rows,
        inverse.reshape(NB, cols, NB),
        (((0, 2), (1, 2)), ((), ())),
        precision=HIGH,
        preferred_element_type=jnp.float32,
    )
    return (normals, factor)


def solution(mesh):
    split = Mesh(mesh.devices.reshape(tuple(SPLIT.values())), tuple(SPLIT))
    in_specs = (P(TRACK, COLS), P(TRACK), P(TRACK), P(), P(), P())
    out_specs = (P(TRACK, COLS), P(TRACK, COLS))
    return jax.shard_map(body, mesh=split, in_specs=in_specs, out_specs=out_specs, check_vma=False)
```

```python
import jax
import jax.numpy as jnp
from jax import lax
from jax.experimental import pallas as pl
from jax.experimental.pallas import tpu as pltpu
from jax.sharding import Mesh
from jax.sharding import PartitionSpec as P

PANEL = 1024
NB = 128
HALF = 64
SUB = 8
BLOCKS = PANEL // NB
LIST = 9
SLICES = 5
NN = (((1,), (0,)), ((), ()))
NT = (((1,), (1,)), ((), ()))
HIGH = lax.Precision.HIGHEST
SPLIT = {"x": 4, "yl": 2, "core": 2, "yh": 2, "z": 4}
TRACK = ("x", "yl", "core")
COLS = ("yh", "z")
PAIRS = ("x", "yl")
CHIPS = ("x", "yl", "yh", "z")
SWAP = [(0, 1), (1, 0)]
VMEM = pl.BlockSpec(memory_space=pltpu.VMEM)
SMEM = pl.BlockSpec(memory_space=pltpu.SMEM)


def gather(x, axis):
    copies = jnp.broadcast_to(x[None], (lax.axis_size(axis),) + x.shape)
    return lax.all_to_all(copies, axis, 0, 0)


def filter_kernel(first_ref, halo_ref, local_ref, start_ref, table_ref, taps_ref, out_ref, ext_ref):
    halo_rows = halo_ref.shape[0]
    row_count, columns = local_ref.shape
    ext_ref[:halo_rows] = halo_ref[...]
    ext_ref[halo_rows : halo_rows + row_count] = local_ref[...]
    ext_ref[halo_rows + row_count :] = jnp.zeros_like(ext_ref[halo_rows + row_count :])
    span = 2 * NB
    taps = taps_ref[...]
    tables = taps.shape[0]
    lane = lax.broadcasted_iota(jnp.int32, (NB, span), 1)
    for b in range(row_count // NB):
        rows = slice(b * NB, (b + 1) * NB)
        choice = lax.broadcasted_iota(jnp.int32, (NB, tables), 1) == table_ref[rows, :]
        row_taps = jnp.dot(
            choice.astype(jnp.float32).astype(jnp.bfloat16), taps, preferred_element_type=jnp.float32
        )
        skewed = pltpu.roll(row_taps, 0, 1, stride=1, stride_axis=0)
        source = first_ref[0] + b * NB - halo_rows + lane
        coefs = jnp.where(source >= start_ref[rows, :], skewed, 0.0).astype(jnp.bfloat16)
        window = ext_ref[b * NB : b * NB + span, :]
        summed = jnp.dot(coefs, window, preferred_element_type=jnp.float32)
        out_ref[:, rows] = summed.T.astype(jnp.bfloat16)


def filter_rows(local, ext_top, seg_start, seg_table, taps, first_row):
    row_count, columns = local.shape
    flipped = jnp.pad(taps[:, ::-1], ((0, 0), (0, 2 * NB - taps.shape[1])))
    return pl.pallas_call(
        filter_kernel,
        out_shape=jax.ShapeDtypeStruct((columns, row_count), jnp.bfloat16),
        in_specs=[SMEM] + [VMEM] * 5,
        out_specs=VMEM,
        scratch_shapes=[pltpu.VMEM((row_count + NB, columns), jnp.bfloat16)],
        compiler_params=pltpu.CompilerParams(vmem_limit_bytes=16 * 2**20),
    )(
        first_row.reshape(1),
        ext_top,
        local,
        seg_start[:, None],
        seg_table[:, None],
        flipped,
    )


def listed(c, h):
    own = (c < BLOCKS // 2) | (h < 2 * (BLOCKS - c))
    if isinstance(c, int):
        return (2 * c + h, c) if own else (7 + h, BLOCKS - 1 - c)
    return jnp.where(own, 2 * c + h, 7 + h), jnp.where(own, c, BLOCKS - 1 - c)


def panel_kernel(turn_ref, ids_ref, ridge_ref, slab_ref, out_ref, panel_ref, picked_ref):
    cols, width, rows = slab_ref.shape
    part = 2 * NB
    lane = lax.broadcasted_iota(jnp.int32, (part, width), 1)
    for p in range(PANEL // part):
        ids = ids_ref[p * part : (p + 1) * part, :]
        acc = jnp.zeros((part, rows), jnp.float32)
        picked = jnp.zeros((part, width), jnp.float32)
        for k in range(cols):
            hit = lane == ids - k * width
            chosen = hit.astype(jnp.float32).astype(jnp.bfloat16)
            acc += jnp.dot(chosen, slab_ref[k], preferred_element_type=jnp.float32)
            picked = jnp.where(hit, ridge_ref[k : k + 1, :], picked)
        total = jnp.sum(picked, axis=1, keepdims=True)
        picked_ref[p * part : (p + 1) * part, :] = jnp.broadcast_to(total, (part, NB))
        panel_ref[p * part : (p + 1) * part, :] = acc.astype(jnp.bfloat16)
    turn = turn_ref[0]
    for h in range(LIST):
        i, j = listed(turn, h)
        left = panel_ref[pl.ds(pl.multiple_of(i * HALF, HALF), HALF), :]
        right = panel_ref[pl.ds(pl.multiple_of(j * NB, NB), NB), :]
        out_ref[h * HALF : (h + 1) * HALF, :] = lax.dot_general(
            left, right, NT, preferred_element_type=jnp.float32
        )
    out_ref[LIST * HALF :, :] = jnp.zeros_like(out_ref[LIST * HALF :, :])


def panel_parts(turn, panel_ids, ridge, slab, track):
    rows = slab.shape[-1]
    return pl.pallas_call(
        panel_kernel,
        out_shape=(
            jax.ShapeDtypeStruct((track * SLICES * SUB, NB), jnp.float32),
            jax.ShapeDtypeStruct((PANEL, rows), jnp.bfloat16),
            jax.ShapeDtypeStruct((PANEL, NB), jnp.float32),
        ),
        in_specs=[SMEM, VMEM, VMEM, VMEM],
        out_specs=(VMEM, VMEM, VMEM),
        compiler_params=pltpu.CompilerParams(vmem_limit_bytes=40 * 2**20),
    )(turn.reshape(1), panel_ids[:, None], ridge.reshape(slab.shape[0], -1), slab)


def halves(a):
    high = a.astype(jnp.bfloat16)
    return high, (a - high.astype(jnp.float32)).astype(jnp.bfloat16)


def product(a, b, dims=NN):
    (ah, al), (bh, bl) = halves(a), halves(b)

    def dot(u, v):
        return lax.dot_general(u, v, dims, preferred_element_type=jnp.float32)

    return dot(ah, bh) + (dot(ah, bl) + dot(al, bh))


def factor_groups(groups, tasks):
    groups = list(groups)
    count = len(groups)
    shape = (SUB, NB)
    lane = lax.broadcasted_iota(jnp.int32, shape, 1)
    sub = lax.broadcasted_iota(jnp.int32, shape, 0)
    share = -(-len(tasks) // count)
    for s in range(count):
        top = groups[s]
        base = s * SUB
        more = s + 1 < count

        def column(g, j):
            return jnp.broadcast_to(groups[g][:, base + j : base + j + 1], shape)

        rows = [jnp.broadcast_to(top[i : i + 1, :], shape) for i in range(SUB)]
        t = {}
        for i in range(SUB):
            for j in range(i + 1):
                t[i, j] = jnp.broadcast_to(rows[i][:, base + j : base + j + 1], shape)
        inside = (lane >= base) & (lane < base + SUB)
        for i in range(SUB):
            rows[i] = jnp.where(inside, (lane == base + i).astype(jnp.float32), rows[i])
        r, u = [], {}
        if more:
            below = [column(s + 1, j) for j in range(SUB)]
            following = jnp.where(inside, 0.0, groups[s + 1])
        for k in range(SUB):
            r.append(1.0 / t[k, k])
            for i in range(k + 1, SUB):
                u[i, k] = t[i, k] * r[k]
            for j in range(k + 1, SUB):
                t[j, j] = t[j, j] - (t[j, k] * t[j, k]) * r[k]
                for i in range(j + 1, SUB):
                    t[i, j] = t[i, j] - u[i, k] * t[j, k]
            for i in range(k + 1, SUB):
                rows[i] = rows[i] - u[i, k] * rows[k]
                if more:
                    below[i] = below[i] - u[i, k] * below[k]
            if more:
                following = following - (below[k] * r[k]) * rows[k]
        packed = rows[0] * lax.rsqrt(t[0, 0])
        for i in range(1, SUB):
            packed = jnp.where(sub == i, rows[i] * lax.rsqrt(t[i, i]), packed)
        groups[s] = packed
        if more:
            groups[s + 1] = following
        if s + 2 < count:
            back = [None] * SUB
            for j in reversed(range(SUB)):
                acc = rows[j] * r[j]
                for i in range(j + 1, SUB):
                    acc = acc - u[i, j] * back[i]
                back[j] = acc
            for g in range(s + 2, count):
                acc = jnp.where(inside, 0.0, groups[g])
                for j in reversed(range(SUB)):
                    acc = acc - column(g, j) * back[j]
                groups[g] = acc
        for task in tasks[s * share : (s + 1) * share]:
            task()
    return groups


def block(i):
    return slice(i * NB, (i + 1) * NB)


def place_pieces(side, ours_ref, theirs_ref, ridge_ref, work_ref):
    chips = ours_ref.shape[0]
    cols = BLOCKS
    for place in range(chips):
        pair, c = divmod(place, cols)
        for core in range(2):
            t = 2 * pair + core
            for e in range(SLICES):
                h, row = divmod(SLICES * t + e, HALF // SUB)
                if h >= LIST:
                    continue
                i, j = listed(c, h)
                here = slice(e * SUB, (e + 1) * SUB)
                value = jnp.where(
                    side == core, ours_ref[place, here, :], theirs_ref[place, here, :]
                )
                first = i * HALF + row * SUB
                work_ref[first : first + SUB, block(j)] = value
    eye = lax.broadcasted_iota(jnp.int32, (NB, NB), 0) == lax.broadcasted_iota(
        jnp.int32, (NB, NB), 1
    )
    for m in range(BLOCKS):
        work_ref[block(m), block(m)] += jnp.where(eye, ridge_ref[block(m), :], 0.0)


def inverse_kernel(place_ref, ours_ref, theirs_ref, ridge_ref, out_ref, work_ref):
    place_pieces(place_ref[1], ours_ref, theirs_ref, ridge_ref, work_ref)
    triangle = lax.broadcasted_iota(jnp.int32, (NB, NB), 0) >= lax.broadcasted_iota(
        jnp.int32, (NB, NB), 1
    )
    tasks = []
    for m in range(BLOCKS):
        groups = [
            work_ref[m * NB + SUB * g : m * NB + SUB * (g + 1), block(m)] for g in range(NB // SUB)
        ]
        groups = factor_groups(groups, tasks)
        inverse = jnp.where(triangle, jnp.concatenate(groups, axis=0), 0.0)
        tasks = []
        left = {}
        if m + 1 < BLOCKS:
            left[m + 1] = product(work_ref[block(m + 1), block(m)], inverse, NT)
            work_ref[block(m + 1), block(m + 1)] -= product(left[m + 1], left[m + 1], NT)

        def finish(m=m, inverse=inverse):
            if m:
                work_ref[block(m), : m * NB] = product(inverse, work_ref[block(m), : m * NB])
            work_ref[block(m), block(m)] = inverse

        def solve(i, m=m, inverse=inverse, left=left):
            left[i] = product(work_ref[block(i), block(m)], inverse, NT)

        def spread(i, m=m, left=left):
            if m:
                work_ref[block(i), : m * NB] -= product(left[i], work_ref[block(m), : m * NB])
            work_ref[block(i), block(m)] = -product(left[i], work_ref[block(m), block(m)])

        def update(i, j, left=left):
            work_ref[block(i), block(j)] -= product(left[i], left[j], NT)

        tasks.append(finish)
        for i in range(m + 1, BLOCKS):
            if i > m + 1:
                tasks.append(lambda i=i, solve=solve: solve(i))
            tasks.append(lambda i=i, spread=spread: spread(i))
            for j in range(m + 1, i + 1):
                if i > m + 1:
                    tasks.append(lambda i=i, j=j, update=update: update(i, j))
    for task in tasks:
        task()
    turn = place_ref[0]
    row = lax.broadcasted_iota(jnp.int32, out_ref.shape, 0) + turn * NB
    col = lax.broadcasted_iota(jnp.int32, out_ref.shape, 1)
    mine = work_ref[pl.ds(pl.multiple_of(turn * NB, NB), NB), :]
    out_ref[...] = jnp.where(row >= col, mine, 0.0)


def inverse_rows(place, ours, theirs, panel_ridge):
    return pl.pallas_call(
        inverse_kernel,
        out_shape=jax.ShapeDtypeStruct((NB, PANEL), jnp.float32),
        in_specs=[SMEM, VMEM, VMEM, VMEM],
        out_specs=VMEM,
        scratch_shapes=[pltpu.VMEM((PANEL, PANEL), jnp.float32)],
        cost_estimate=pl.CostEstimate(flops=38 * 10**9, transcendentals=4 * PANEL, bytes_accessed=6 * 2**20),
        compiler_params=pltpu.CompilerParams(vmem_limit_bytes=40 * 2**20),
    )(place, ours, theirs, panel_ridge)


def body(design, seg_start, seg_table, taps, ridge, col_perm):
    row_count, width = design.shape
    halo_rows = taps.shape[1] - 1
    track, cols = lax.axis_size(TRACK), lax.axis_size(COLS)
    t, c, core = lax.axis_index(TRACK), lax.axis_index(COLS), lax.axis_index("core")
    slab = width * cols
    row_blk = slab // track
    panel_ids = col_perm[:PANEL]

    pairs = [(i, i + 1) for i in range(track - 1)]
    ext_top = lax.ppermute(design[row_count - halo_rows :], TRACK, pairs)
    filtered = filter_rows(design, ext_top, seg_start, seg_table, taps, t * row_count)
    gathered = gather(filtered, COLS)

    block_part, panel, panel_ridge = panel_parts(c, panel_ids, ridge, gathered, track)
    slab_rows, block_part = lax.optimization_barrier((gathered, block_part))
    slab_rows = slab_rows.reshape(track // 2, 2, row_blk, row_count)
    block_parts = lax.all_to_all(block_part.reshape(track, SLICES * SUB, NB), TRACK, 0, 0)

    def rows_of(side):
        rows = lax.dynamic_index_in_dim(slab_rows, side, 1, keepdims=False)
        return lax.dot_general(
            rows, filtered, (((2,), (1,)), ((), ())), preferred_element_type=jnp.float32
        )

    sent, block_sum = lax.optimization_barrier((rows_of(1 - core), jnp.sum(block_parts, axis=0)))
    ours = gather(block_sum, CHIPS)
    sums = rows_of(core) + lax.ppermute(sent, "core", SWAP)
    narrow, ours = lax.optimization_barrier((sums.astype(jnp.float16), ours))
    theirs = lax.ppermute(ours, "core", SWAP)
    parts = lax.all_to_all(narrow, PAIRS, 0, 0)
    inverse = inverse_rows(jnp.stack([c, core]), ours, theirs, panel_ridge)

    whitened = lax.dot_general(
        inverse, panel.astype(jnp.float32), NN, precision=HIGH, preferred_element_type=jnp.float32
    )
    high, low = halves(whitened)
    slab_all = gathered.reshape(slab, row_count)
    factor_part = lax.dot_general(slab_all, high, NT, preferred_element_type=jnp.float32)
    factor_part += lax.dot_general(slab_all, low, NT, preferred_element_type=jnp.float32)
    factor_part = factor_part.astype(jnp.float16).reshape(track, row_blk, NB)
    factor_parts = lax.all_to_all(factor_part, TRACK, 0, 0)
    row_ids = t * row_blk + jnp.arange(row_blk, dtype=jnp.int32)
    row_ridge = lax.dynamic_slice_in_dim(ridge, t * row_blk, row_blk)
    spread = jnp.where(row_ids[:, None] == panel_ids[None, :], row_ridge[:, None], 0.0)
    ridge_part = lax.dot_general(
        spread, inverse, NT, precision=HIGH, preferred_element_type=jnp.float32
    )
    factor = jnp.sum(factor_parts.astype(jnp.float32), axis=0) + ridge_part

    col_ids = c * width + jnp.arange(width, dtype=jnp.int32)
    normals = jnp.sum(parts.astype(jnp.float32), axis=0) + jnp.where(
        row_ids[:, None] == col_ids[None, :], row_ridge[:, None], 0.0
    )
    return (normals, factor)


def solution(mesh):
    split = Mesh(mesh.devices.reshape(tuple(SPLIT.values())), tuple(SPLIT))
    in_specs = (P(TRACK, COLS), P(TRACK), P(TRACK), P(), P(), P())
    out_specs = (P(TRACK, COLS), P(TRACK, COLS))
    return jax.shard_map(body, mesh=split, in_specs=in_specs, out_specs=out_specs, check_vma=False)
```

```python
import jax
import jax.numpy as jnp
from jax import lax
from jax.experimental import pallas as pl
from jax.experimental.pallas import tpu as pltpu
from jax.sharding import Mesh
from jax.sharding import PartitionSpec as P

PANEL = 1024
NB = 128
HALF = 64
SUB = 8
BLOCKS = PANEL // NB
LIST = 9
SLICES = 5
NN = (((1,), (0,)), ((), ()))
NT = (((1,), (1,)), ((), ()))
HIGH = lax.Precision.HIGHEST
SPLIT = {"x": 4, "yl": 2, "core": 2, "yh": 2, "z": 4}
TRACK = ("x", "yl", "core")
COLS = ("yh", "z")
PAIRS = ("x", "yl")
CHIPS = ("x", "yl", "yh", "z")
SWAP = [(0, 1), (1, 0)]
VMEM = pl.BlockSpec(memory_space=pltpu.VMEM)
SMEM = pl.BlockSpec(memory_space=pltpu.SMEM)


def gather(x, axis):
    copies = jnp.broadcast_to(x[None], (lax.axis_size(axis),) + x.shape)
    return lax.all_to_all(copies, axis, 0, 0)


def filter_kernel(first_ref, halo_ref, local_ref, start_ref, table_ref, taps_ref, out_ref, ext_ref):
    halo_rows = halo_ref.shape[0]
    row_count, columns = local_ref.shape
    ext_ref[:halo_rows] = halo_ref[...]
    ext_ref[halo_rows : halo_rows + row_count] = local_ref[...]
    ext_ref[halo_rows + row_count :] = jnp.zeros_like(ext_ref[halo_rows + row_count :])
    span = 2 * NB
    taps = taps_ref[...]
    tables = taps.shape[0]
    lane = lax.broadcasted_iota(jnp.int32, (NB, span), 1)
    for b in range(row_count // NB):
        rows = slice(b * NB, (b + 1) * NB)
        choice = lax.broadcasted_iota(jnp.int32, (NB, tables), 1) == table_ref[rows, :]
        row_taps = jnp.dot(
            choice.astype(jnp.float32).astype(jnp.bfloat16), taps, preferred_element_type=jnp.float32
        )
        skewed = pltpu.roll(row_taps, 0, 1, stride=1, stride_axis=0)
        source = first_ref[0] + b * NB - halo_rows + lane
        coefs = jnp.where(source >= start_ref[rows, :], skewed, 0.0).astype(jnp.bfloat16)
        window = ext_ref[b * NB : b * NB + span, :]
        summed = jnp.dot(coefs, window, preferred_element_type=jnp.float32)
        out_ref[:, rows] = summed.T.astype(jnp.bfloat16)


def filter_rows(local, ext_top, seg_start, seg_table, taps, first_row):
    row_count, columns = local.shape
    flipped = jnp.pad(taps[:, ::-1], ((0, 0), (0, 2 * NB - taps.shape[1])))
    return pl.pallas_call(
        filter_kernel,
        out_shape=jax.ShapeDtypeStruct((columns, row_count), jnp.bfloat16),
        in_specs=[SMEM] + [VMEM] * 5,
        out_specs=VMEM,
        scratch_shapes=[pltpu.VMEM((row_count + NB, columns), jnp.bfloat16)],
        compiler_params=pltpu.CompilerParams(vmem_limit_bytes=16 * 2**20),
    )(
        first_row.reshape(1),
        ext_top,
        local,
        seg_start[:, None],
        seg_table[:, None],
        flipped,
    )


def listed(c, h):
    own = (c < BLOCKS // 2) | (h < 2 * (BLOCKS - c))
    if isinstance(c, int):
        return (2 * c + h, c) if own else (7 + h, BLOCKS - 1 - c)
    return jnp.where(own, 2 * c + h, 7 + h), jnp.where(own, c, BLOCKS - 1 - c)


def panel_kernel(turn_ref, ids_ref, slab_ref, out_ref, panel_ref):
    cols, width, rows = slab_ref.shape
    part = 2 * NB
    lane = lax.broadcasted_iota(jnp.int32, (part, width), 1)
    for p in range(PANEL // part):
        ids = ids_ref[p * part : (p + 1) * part, :]
        acc = jnp.zeros((part, rows), jnp.float32)
        for k in range(cols):
            chosen = (lane == ids - k * width).astype(jnp.float32).astype(jnp.bfloat16)
            acc += jnp.dot(chosen, slab_ref[k], preferred_element_type=jnp.float32)
        panel_ref[p * part : (p + 1) * part, :] = acc.astype(jnp.bfloat16)
    turn = turn_ref[0]
    for h in range(LIST):
        i, j = listed(turn, h)
        left = panel_ref[pl.ds(pl.multiple_of(i * HALF, HALF), HALF), :]
        right = panel_ref[pl.ds(pl.multiple_of(j * NB, NB), NB), :]
        out_ref[h * HALF : (h + 1) * HALF, :] = lax.dot_general(
            left, right, NT, preferred_element_type=jnp.float32
        )
    out_ref[LIST * HALF :, :] = jnp.zeros_like(out_ref[LIST * HALF :, :])


def panel_parts(turn, panel_ids, slab, track):
    rows = slab.shape[-1]
    return pl.pallas_call(
        panel_kernel,
        out_shape=(
            jax.ShapeDtypeStruct((track * SLICES * SUB, NB), jnp.float32),
            jax.ShapeDtypeStruct((PANEL, rows), jnp.bfloat16),
        ),
        in_specs=[SMEM, VMEM, VMEM],
        out_specs=(VMEM, VMEM),
        compiler_params=pltpu.CompilerParams(vmem_limit_bytes=40 * 2**20),
    )(turn.reshape(1), panel_ids[:, None], slab)


def halves(a):
    high = a.astype(jnp.bfloat16)
    return high, (a - high.astype(jnp.float32)).astype(jnp.bfloat16)


def product(a, b, dims=NN):
    (ah, al), (bh, bl) = halves(a), halves(b)

    def dot(u, v):
        return lax.dot_general(u, v, dims, preferred_element_type=jnp.float32)

    return dot(ah, bh) + (dot(ah, bl) + dot(al, bh))


def factor_groups(groups, tasks):
    groups = list(groups)
    count = len(groups)
    shape = (SUB, NB)
    lane = lax.broadcasted_iota(jnp.int32, shape, 1)
    sub = lax.broadcasted_iota(jnp.int32, shape, 0)
    share = -(-len(tasks) // count)
    for s in range(count):
        top = groups[s]
        base = s * SUB
        more = s + 1 < count

        def column(g, j):
            return jnp.broadcast_to(groups[g][:, base + j : base + j + 1], shape)

        rows = [jnp.broadcast_to(top[i : i + 1, :], shape) for i in range(SUB)]
        t = {}
        for i in range(SUB):
            for j in range(i + 1):
                t[i, j] = jnp.broadcast_to(rows[i][:, base + j : base + j + 1], shape)
        inside = (lane >= base) & (lane < base + SUB)
        for i in range(SUB):
            rows[i] = jnp.where(inside, (lane == base + i).astype(jnp.float32), rows[i])
        r, u = [], {}
        if more:
            below = [column(s + 1, j) for j in range(SUB)]
            following = jnp.where(inside, 0.0, groups[s + 1])
        for k in range(0, SUB, 2):
            n = k + 1
            a, b = t[k, k], t[n, k]
            r.append(1.0 / a)
            r.append(a * (1.0 / (a * t[n, n] - b * b)))
            for i in range(n, SUB):
                u[i, k] = t[i, k] * r[k]
            t[n, n] = t[n, n] - b * u[n, k]
            for i in range(n + 1, SUB):
                t[i, n] = t[i, n] - u[i, k] * b
                u[i, n] = t[i, n] * r[n]
            for j in range(n + 1, SUB):
                for i in range(j, SUB):
                    t[i, j] = (t[i, j] - u[i, k] * t[j, k]) - u[i, n] * t[j, n]
            for q in (k, n):
                for i in range(q + 1, SUB):
                    rows[i] = rows[i] - u[i, q] * rows[q]
                    if more:
                        below[i] = below[i] - u[i, q] * below[q]
                if more:
                    following = following - (below[q] * r[q]) * rows[q]
        scale = [lax.rsqrt(t[i, i]) for i in range(SUB)]
        packed = rows[0] * scale[0]
        for i in range(1, SUB):
            packed = jnp.where(sub == i, rows[i] * scale[i], packed)
        groups[s] = packed
        if more:
            groups[s + 1] = following
        if s + 2 < count:
            back = [None] * SUB
            for j in reversed(range(SUB)):
                acc = rows[j] * r[j]
                for i in range(j + 1, SUB):
                    acc = acc - u[i, j] * back[i]
                back[j] = acc
            for g in range(s + 2, count):
                acc = jnp.where(inside, 0.0, groups[g])
                for j in reversed(range(SUB)):
                    acc = acc - column(g, j) * back[j]
                groups[g] = acc
        for task in tasks[s * share : (s + 1) * share]:
            task()
    return groups


def block(i):
    return slice(i * NB, (i + 1) * NB)


def place_pieces(side, ours_ref, theirs_ref, ridge_ref, work_ref):
    chips = ours_ref.shape[0]
    cols = BLOCKS
    for place in range(chips):
        pair, c = divmod(place, cols)
        for core in range(2):
            t = 2 * pair + core
            for e in range(SLICES):
                h, row = divmod(SLICES * t + e, HALF // SUB)
                if h >= LIST:
                    continue
                i, j = listed(c, h)
                here = slice(e * SUB, (e + 1) * SUB)
                value = jnp.where(
                    side == core, ours_ref[place, here, :], theirs_ref[place, here, :]
                )
                first = i * HALF + row * SUB
                work_ref[first : first + SUB, block(j)] = value
    eye = lax.broadcasted_iota(jnp.int32, (NB, NB), 0) == lax.broadcasted_iota(
        jnp.int32, (NB, NB), 1
    )
    for m in range(BLOCKS):
        work_ref[block(m), block(m)] += jnp.where(eye, ridge_ref[:, block(m)], 0.0)


def inverse_kernel(
    place_ref,
    ours_ref,
    theirs_ref,
    ridge_ref,
    panel_ref,
    slab_ref,
    out_ref,
    kept_ref,
    sent_ref,
    work_ref,
):
    place_pieces(place_ref[1], ours_ref, theirs_ref, ridge_ref, work_ref)
    triangle = lax.broadcasted_iota(jnp.int32, (NB, NB), 0) >= lax.broadcasted_iota(
        jnp.int32, (NB, NB), 1
    )
    tasks = []
    for m in range(BLOCKS):
        groups = [
            work_ref[m * NB + SUB * g : m * NB + SUB * (g + 1), block(m)] for g in range(NB // SUB)
        ]
        groups = factor_groups(groups, tasks)
        inverse = jnp.where(triangle, jnp.concatenate(groups, axis=0), 0.0)
        tasks = []
        left = {}
        if m + 1 < BLOCKS:
            left[m + 1] = product(work_ref[block(m + 1), block(m)], inverse, NT)
            work_ref[block(m + 1), block(m + 1)] -= product(left[m + 1], left[m + 1], NT)

        def finish(m=m, inverse=inverse):
            if m:
                work_ref[block(m), : m * NB] = product(inverse, work_ref[block(m), : m * NB])
            work_ref[block(m), block(m)] = inverse

        def solve(i, m=m, inverse=inverse, left=left):
            left[i] = product(work_ref[block(i), block(m)], inverse, NT)

        def spread(i, m=m, left=left):
            if m:
                work_ref[block(i), : m * NB] -= product(left[i], work_ref[block(m), : m * NB])
            work_ref[block(i), block(m)] = -product(left[i], work_ref[block(m), block(m)])

        def update(i, j, left=left):
            work_ref[block(i), block(j)] -= product(left[i], left[j], NT)

        tasks.append(finish)
        for i in range(m + 1, BLOCKS):
            if i > m + 1:
                tasks.append(lambda i=i, solve=solve: solve(i))
            tasks.append(lambda i=i, spread=spread: spread(i))
            for j in range(m + 1, i + 1):
                if i > m + 1:
                    tasks.append(lambda i=i, j=j, update=update: update(i, j))
    for task in tasks:
        task()
    turn = place_ref[0]
    row = lax.broadcasted_iota(jnp.int32, out_ref.shape, 0) + turn * NB
    col = lax.broadcasted_iota(jnp.int32, out_ref.shape, 1)
    mine = work_ref[pl.ds(pl.multiple_of(turn * NB, NB), NB), :]
    mine = jnp.where(row >= col, mine, 0.0)
    out_ref[...] = mine
    panel = panel_ref[...]
    whitened = sum(jnp.dot(x, panel, preferred_element_type=jnp.float32) for x in halves(mine))
    both = jnp.concatenate(halves(whitened), axis=0)
    count, row_blk, _ = kept_ref.shape
    for side, part_ref in ((place_ref[1], kept_ref), (1 - place_ref[1], sent_ref)):
        for k in range(count):
            rows = slab_ref[k, pl.ds(pl.multiple_of(side * row_blk, row_blk), row_blk), :]
            twice = lax.dot_general(rows, both, NT, preferred_element_type=jnp.float32)
            part_ref[k] = twice[:, :NB] + twice[:, NB:]


def inverse_rows(place, ours, theirs, panel_ridge, panel, slab):
    count, width, _ = slab.shape
    part = jax.ShapeDtypeStruct((count, width // 2, NB), jnp.float32)
    return pl.pallas_call(
        inverse_kernel,
        out_shape=(
            jax.ShapeDtypeStruct((NB, PANEL), jnp.float32),
            part,
            part,
        ),
        in_specs=[SMEM] + [VMEM] * 5,
        out_specs=(VMEM, VMEM, VMEM),
        scratch_shapes=[pltpu.VMEM((PANEL, PANEL), jnp.float32)],
        cost_estimate=pl.CostEstimate(
            flops=38 * 10**9, transcendentals=4 * PANEL, bytes_accessed=12 * 2**20
        ),
        compiler_params=pltpu.CompilerParams(vmem_limit_bytes=48 * 2**20),
    )(place, ours, theirs, panel_ridge[None, :], panel, slab)


def body(design, seg_start, seg_table, taps, ridge, col_perm):
    row_count, width = design.shape
    halo_rows = taps.shape[1] - 1
    track, cols = lax.axis_size(TRACK), lax.axis_size(COLS)
    t, c, core = lax.axis_index(TRACK), lax.axis_index(COLS), lax.axis_index("core")
    slab = width * cols
    row_blk = slab // track
    panel_ids = col_perm[:PANEL]

    pairs = [(i, i + 1) for i in range(track - 1)]
    ext_top = lax.ppermute(design[row_count - halo_rows :], TRACK, pairs)
    filtered = filter_rows(design, ext_top, seg_start, seg_table, taps, t * row_count)
    gathered = gather(filtered, COLS)

    block_part, panel = panel_parts(c, panel_ids, gathered, track)
    slab_rows, block_part = lax.optimization_barrier((gathered, block_part))
    slab_rows = slab_rows.reshape(track // 2, 2, row_blk, row_count)
    block_parts = lax.all_to_all(block_part.reshape(track, SLICES * SUB, NB), TRACK, 0, 0)

    def rows_of(side):
        rows = lax.dynamic_index_in_dim(slab_rows, side, 1, keepdims=False)
        return lax.dot_general(
            rows, filtered, (((2,), (1,)), ((), ())), preferred_element_type=jnp.float32
        )

    sent, block_sum = lax.optimization_barrier((rows_of(1 - core), jnp.sum(block_parts, axis=0)))
    ours = gather(block_sum, CHIPS)
    late_ids, _ = lax.optimization_barrier((panel_ids, block_sum))
    panel_ridge = jnp.take(ridge, late_ids)
    sums = rows_of(core) + lax.ppermute(sent, "core", SWAP)
    narrow, ours, panel_ridge = lax.optimization_barrier(
        (sums.astype(jnp.float16), ours, panel_ridge)
    )
    theirs = lax.ppermute(ours, "core", SWAP)
    parts = lax.all_to_all(narrow, PAIRS, 0, 0)
    inverse, kept, sent = inverse_rows(
        jnp.stack([c, core]), ours, theirs, panel_ridge, panel, gathered
    )
    factor_part = (kept + lax.ppermute(sent, "core", SWAP)).astype(jnp.float16)
    factor_parts = lax.all_to_all(factor_part, PAIRS, 0, 0)
    row_ids = t * row_blk + jnp.arange(row_blk, dtype=jnp.int32)
    row_ridge = lax.dynamic_slice_in_dim(ridge, t * row_blk, row_blk)
    spread = jnp.where(row_ids[:, None] == panel_ids[None, :], row_ridge[:, None], 0.0)
    ridge_part = lax.dot_general(
        spread, inverse, NT, precision=HIGH, preferred_element_type=jnp.float32
    )
    factor = jnp.sum(factor_parts.astype(jnp.float32), axis=0) + ridge_part

    col_ids = c * width + jnp.arange(width, dtype=jnp.int32)
    normals = jnp.sum(parts.astype(jnp.float32), axis=0) + jnp.where(
        row_ids[:, None] == col_ids[None, :], row_ridge[:, None], 0.0
    )
    return (normals, factor)


def solution(mesh):
    split = Mesh(mesh.devices.reshape(tuple(SPLIT.values())), tuple(SPLIT))
    in_specs = (P(TRACK, COLS), P(TRACK), P(TRACK), P(), P(), P())
    out_specs = (P(TRACK, COLS), P(TRACK, COLS))
    return jax.shard_map(body, mesh=split, in_specs=in_specs, out_specs=out_specs, check_vma=False)
```

```python
import jax
import jax.numpy as jnp
from jax import lax
from jax.experimental import pallas as pl
from jax.experimental.pallas import tpu as pltpu
from jax.sharding import Mesh
from jax.sharding import PartitionSpec as P

PANEL = 1024
NB = 128
HALF = 64
SUB = 8
BLOCKS = PANEL // NB
LIST = 9
SLICES = 5
NN = (((1,), (0,)), ((), ()))
NT = (((1,), (1,)), ((), ()))
HIGH = lax.Precision.HIGHEST
SPLIT = {"x": 4, "yl": 2, "core": 2, "yh": 2, "z": 4}
TRACK = ("x", "yl", "core")
COLS = ("yh", "z")
PAIRS = ("x", "yl")
CHIPS = ("x", "yl", "yh", "z")
SWAP = [(0, 1), (1, 0)]
VMEM = pl.BlockSpec(memory_space=pltpu.VMEM)
SMEM = pl.BlockSpec(memory_space=pltpu.SMEM)


def gather(x, axis):
    copies = jnp.broadcast_to(x[None], (lax.axis_size(axis),) + x.shape)
    return lax.all_to_all(copies, axis, 0, 0)


def filter_kernel(first_ref, halo_ref, local_ref, start_ref, table_ref, taps_ref, out_ref, ext_ref):
    halo_rows = halo_ref.shape[0]
    row_count, columns = local_ref.shape
    ext_ref[:halo_rows] = halo_ref[...]
    ext_ref[halo_rows : halo_rows + row_count] = local_ref[...]
    ext_ref[halo_rows + row_count :] = jnp.zeros_like(ext_ref[halo_rows + row_count :])
    span = 2 * NB
    taps = taps_ref[...]
    tables = taps.shape[0]
    lane = lax.broadcasted_iota(jnp.int32, (NB, span), 1)
    for b in range(row_count // NB):
        rows = slice(b * NB, (b + 1) * NB)
        choice = lax.broadcasted_iota(jnp.int32, (NB, tables), 1) == table_ref[rows, :]
        row_taps = jnp.dot(
            choice.astype(jnp.float32).astype(jnp.bfloat16), taps, preferred_element_type=jnp.float32
        )
        skewed = pltpu.roll(row_taps, 0, 1, stride=1, stride_axis=0)
        source = first_ref[0] + b * NB - halo_rows + lane
        coefs = jnp.where(source >= start_ref[rows, :], skewed, 0.0).astype(jnp.bfloat16)
        window = ext_ref[b * NB : b * NB + span, :]
        summed = jnp.dot(coefs, window, preferred_element_type=jnp.float32)
        out_ref[:, rows] = summed.T.astype(jnp.bfloat16)


def filter_rows(local, ext_top, seg_start, seg_table, taps, first_row):
    row_count, columns = local.shape
    flipped = jnp.pad(taps[:, ::-1], ((0, 0), (0, 2 * NB - taps.shape[1])))
    return pl.pallas_call(
        filter_kernel,
        out_shape=jax.ShapeDtypeStruct((columns, row_count), jnp.bfloat16),
        in_specs=[SMEM] + [VMEM] * 5,
        out_specs=VMEM,
        scratch_shapes=[pltpu.VMEM((row_count + NB, columns), jnp.bfloat16)],
        compiler_params=pltpu.CompilerParams(vmem_limit_bytes=16 * 2**20),
    )(
        first_row.reshape(1),
        ext_top,
        local,
        seg_start[:, None],
        seg_table[:, None],
        flipped,
    )


def listed(c, h):
    own = (c < BLOCKS // 2) | (h < 2 * (BLOCKS - c))
    if isinstance(c, int):
        return (2 * c + h, c) if own else (7 + h, BLOCKS - 1 - c)
    return jnp.where(own, 2 * c + h, 7 + h), jnp.where(own, c, BLOCKS - 1 - c)


def panel_kernel(turn_ref, ids_ref, slab_ref, out_ref, panel_ref):
    cols, width, rows = slab_ref.shape
    part = 2 * NB
    lane = lax.broadcasted_iota(jnp.int32, (part, width), 1)
    for p in range(PANEL // part):
        ids = ids_ref[p * part : (p + 1) * part, :]
        acc = jnp.zeros((part, rows), jnp.float32)
        for k in range(cols):
            chosen = (lane == ids - k * width).astype(jnp.float32).astype(jnp.bfloat16)
            acc += jnp.dot(chosen, slab_ref[k], preferred_element_type=jnp.float32)
        panel_ref[p * part : (p + 1) * part, :] = acc.astype(jnp.bfloat16)
    turn = turn_ref[0]
    for h in range(LIST):
        i, j = listed(turn, h)
        left = panel_ref[pl.ds(pl.multiple_of(i * HALF, HALF), HALF), :]
        right = panel_ref[pl.ds(pl.multiple_of(j * NB, NB), NB), :]
        out_ref[h * HALF : (h + 1) * HALF, :] = lax.dot_general(
            left, right, NT, preferred_element_type=jnp.float32
        )
    out_ref[LIST * HALF :, :] = jnp.zeros_like(out_ref[LIST * HALF :, :])


def panel_parts(turn, panel_ids, slab, track):
    rows = slab.shape[-1]
    return pl.pallas_call(
        panel_kernel,
        out_shape=(
            jax.ShapeDtypeStruct((track * SLICES * SUB, NB), jnp.float32),
            jax.ShapeDtypeStruct((PANEL, rows), jnp.bfloat16),
        ),
        in_specs=[SMEM, VMEM, VMEM],
        out_specs=(VMEM, VMEM),
        compiler_params=pltpu.CompilerParams(vmem_limit_bytes=20 * 2**20),
    )(turn.reshape(1), panel_ids[:, None], slab)


def halves(a):
    high = a.astype(jnp.bfloat16)
    return high, (a - high.astype(jnp.float32)).astype(jnp.bfloat16)


def product(a, b, dims=NN):
    (ah, al), (bh, bl) = halves(a), halves(b)

    def dot(u, v):
        return lax.dot_general(u, v, dims, preferred_element_type=jnp.float32)

    return dot(ah, bh) + (dot(ah, bl) + dot(al, bh))


def reciprocal(x):
    guess = pl.reciprocal(x, approx=True)
    return guess * (2.0 - x * guess)


def factor_groups(groups, tasks):
    groups = list(groups)
    count = len(groups)
    shape = (SUB, NB)
    lane = lax.broadcasted_iota(jnp.int32, shape, 1)
    sub = lax.broadcasted_iota(jnp.int32, shape, 0)
    share = -(-len(tasks) // count)
    for s in range(count):
        top = groups[s]
        base = s * SUB
        more = s + 1 < count

        def column(g, j):
            return jnp.broadcast_to(groups[g][:, base + j : base + j + 1], shape)

        rows = [jnp.broadcast_to(top[i : i + 1, :], shape) for i in range(SUB)]
        t = {}
        for i in range(SUB):
            for j in range(i + 1):
                t[i, j] = jnp.broadcast_to(rows[i][:, base + j : base + j + 1], shape)
        inside = (lane >= base) & (lane < base + SUB)
        for i in range(SUB):
            rows[i] = jnp.where(inside, (lane == base + i).astype(jnp.float32), rows[i])
        r, u = [], {}
        if more:
            below = [column(s + 1, j) for j in range(SUB)]
            following = jnp.where(inside, 0.0, groups[s + 1])
        for k in range(0, SUB, 2):
            n = k + 1
            a, b = t[k, k], t[n, k]
            r.append(reciprocal(a))
            r.append(a * reciprocal(a * t[n, n] - b * b))
            for i in range(n, SUB):
                u[i, k] = t[i, k] * r[k]
            t[n, n] = t[n, n] - b * u[n, k]
            for i in range(n + 1, SUB):
                t[i, n] = t[i, n] - u[i, k] * b
                u[i, n] = t[i, n] * r[n]
            for j in range(n + 1, SUB):
                for i in range(j, SUB):
                    t[i, j] = (t[i, j] - u[i, k] * t[j, k]) - u[i, n] * t[j, n]
            for q in (k, n):
                for i in range(q + 1, SUB):
                    rows[i] = rows[i] - u[i, q] * rows[q]
                    if more:
                        below[i] = below[i] - u[i, q] * below[q]
                if more:
                    following = following - (below[q] * r[q]) * rows[q]
        scale = [lax.rsqrt(t[i, i]) for i in range(SUB)]
        packed = rows[0] * scale[0]
        for i in range(1, SUB):
            packed = jnp.where(sub == i, rows[i] * scale[i], packed)
        groups[s] = packed
        if more:
            groups[s + 1] = following
        if s + 2 < count:
            back = [None] * SUB
            for j in reversed(range(SUB)):
                acc = rows[j] * r[j]
                for i in range(j + 1, SUB):
                    acc = acc - u[i, j] * back[i]
                back[j] = acc
            for g in range(s + 2, count):
                acc = jnp.where(inside, 0.0, groups[g])
                for j in reversed(range(SUB)):
                    acc = acc - column(g, j) * back[j]
                groups[g] = acc
        for task in tasks[s * share : (s + 1) * share]:
            task()
    return groups


def block(i):
    return slice(i * NB, (i + 1) * NB)


def place_pieces(side, ours_ref, theirs_ref, ridge_ref, work_ref):
    chips = ours_ref.shape[0]
    cols = BLOCKS
    for place in range(chips):
        pair, c = divmod(place, cols)
        for core in range(2):
            t = 2 * pair + core
            for e in range(SLICES):
                h, row = divmod(SLICES * t + e, HALF // SUB)
                if h >= LIST:
                    continue
                i, j = listed(c, h)
                here = slice(e * SUB, (e + 1) * SUB)
                value = jnp.where(
                    side == core, ours_ref[place, here, :], theirs_ref[place, here, :]
                )
                first = i * HALF + row * SUB
                work_ref[first : first + SUB, block(j)] = value
    eye = lax.broadcasted_iota(jnp.int32, (NB, NB), 0) == lax.broadcasted_iota(
        jnp.int32, (NB, NB), 1
    )
    for m in range(BLOCKS):
        work_ref[block(m), block(m)] += jnp.where(eye, ridge_ref[:, block(m)], 0.0)


def inverse_kernel(
    place_ref,
    ours_ref,
    theirs_ref,
    ridge_ref,
    panel_ref,
    slab_ref,
    out_ref,
    kept_ref,
    sent_ref,
    work_ref,
):
    place_pieces(place_ref[1], ours_ref, theirs_ref, ridge_ref, work_ref)
    triangle = lax.broadcasted_iota(jnp.int32, (NB, NB), 0) >= lax.broadcasted_iota(
        jnp.int32, (NB, NB), 1
    )
    tasks = []
    for m in range(BLOCKS):
        groups = [
            work_ref[m * NB + SUB * g : m * NB + SUB * (g + 1), block(m)] for g in range(NB // SUB)
        ]
        groups = factor_groups(groups, tasks)
        inverse = jnp.where(triangle, jnp.concatenate(groups, axis=0), 0.0)
        tasks = []
        left = {}
        if m + 1 < BLOCKS:
            left[m + 1] = product(work_ref[block(m + 1), block(m)], inverse, NT)
            work_ref[block(m + 1), block(m + 1)] -= product(left[m + 1], left[m + 1], NT)

        def finish(m=m, inverse=inverse):
            if m:
                work_ref[block(m), : m * NB] = product(inverse, work_ref[block(m), : m * NB])
            work_ref[block(m), block(m)] = inverse

        def solve(i, m=m, inverse=inverse, left=left):
            left[i] = product(work_ref[block(i), block(m)], inverse, NT)

        def spread(i, m=m, left=left):
            if m:
                work_ref[block(i), : m * NB] -= product(left[i], work_ref[block(m), : m * NB])
            work_ref[block(i), block(m)] = -product(left[i], work_ref[block(m), block(m)])

        def update(i, j, left=left):
            work_ref[block(i), block(j)] -= product(left[i], left[j], NT)

        tasks.append(finish)
        for i in range(m + 1, BLOCKS):
            if i > m + 1:
                tasks.append(lambda i=i, solve=solve: solve(i))
            tasks.append(lambda i=i, spread=spread: spread(i))
            for j in range(m + 1, i + 1):
                if i > m + 1:
                    tasks.append(lambda i=i, j=j, update=update: update(i, j))
    for task in tasks:
        task()
    turn = place_ref[0]
    row = lax.broadcasted_iota(jnp.int32, out_ref.shape, 0) + turn * NB
    col = lax.broadcasted_iota(jnp.int32, out_ref.shape, 1)
    mine = work_ref[pl.ds(pl.multiple_of(turn * NB, NB), NB), :]
    mine = jnp.where(row >= col, mine, 0.0)
    out_ref[...] = mine
    panel = panel_ref[...]
    whitened = sum(jnp.dot(x, panel, preferred_element_type=jnp.float32) for x in halves(mine))
    both = jnp.concatenate(halves(whitened), axis=0)
    count, row_blk, _ = kept_ref.shape
    for side, part_ref in ((place_ref[1], kept_ref), (1 - place_ref[1], sent_ref)):
        for k in range(count):
            rows = slab_ref[k, pl.ds(pl.multiple_of(side * row_blk, row_blk), row_blk), :]
            twice = lax.dot_general(rows, both, NT, preferred_element_type=jnp.float32)
            part_ref[k] = twice[:, :NB] + twice[:, NB:]


def inverse_rows(place, ours, theirs, panel_ridge, panel, slab):
    count, width, _ = slab.shape
    part = jax.ShapeDtypeStruct((count, width // 2, NB), jnp.float32)
    return pl.pallas_call(
        inverse_kernel,
        out_shape=(
            jax.ShapeDtypeStruct((NB, PANEL), jnp.float32),
            part,
            part,
        ),
        in_specs=[SMEM] + [VMEM] * 5,
        out_specs=(VMEM, VMEM, VMEM),
        scratch_shapes=[pltpu.VMEM((PANEL, PANEL), jnp.float32)],
        cost_estimate=pl.CostEstimate(
            flops=38 * 10**9, transcendentals=4 * PANEL, bytes_accessed=12 * 2**20
        ),
        compiler_params=pltpu.CompilerParams(vmem_limit_bytes=24 * 2**20),
    )(place, ours, theirs, panel_ridge[None, :], panel, slab)


def body(design, seg_start, seg_table, taps, ridge, col_perm):
    row_count, width = design.shape
    halo_rows = taps.shape[1] - 1
    track, cols = lax.axis_size(TRACK), lax.axis_size(COLS)
    t, c, core = lax.axis_index(TRACK), lax.axis_index(COLS), lax.axis_index("core")
    slab = width * cols
    row_blk = slab // track
    panel_ids = col_perm[:PANEL]

    pairs = [(i, i + 1) for i in range(track - 1)]
    ext_top = lax.ppermute(design[row_count - halo_rows :], TRACK, pairs)
    filtered = filter_rows(design, ext_top, seg_start, seg_table, taps, t * row_count)
    gathered = gather(filtered, COLS)

    block_part, panel = panel_parts(c, panel_ids, gathered, track)
    slab_rows, block_part = lax.optimization_barrier((gathered, block_part))
    slab_rows = slab_rows.reshape(track // 2, 2, row_blk, row_count)
    block_parts = lax.all_to_all(block_part.reshape(track, SLICES * SUB, NB), TRACK, 0, 0)

    def rows_of(side):
        rows = lax.dynamic_index_in_dim(slab_rows, side, 1, keepdims=False)
        return lax.dot_general(
            rows, filtered, (((2,), (1,)), ((), ())), preferred_element_type=jnp.float32
        )

    sent, block_sum = lax.optimization_barrier((rows_of(1 - core), jnp.sum(block_parts, axis=0)))
    ours = gather(block_sum, CHIPS)
    late_ids, _ = lax.optimization_barrier((panel_ids, block_sum))
    panel_ridge = jnp.take(ridge, late_ids)
    sums = rows_of(core) + lax.ppermute(sent, "core", SWAP)
    narrow, ours, panel_ridge = lax.optimization_barrier(
        (sums.astype(jnp.float16), ours, panel_ridge)
    )
    theirs = lax.ppermute(ours, "core", SWAP)
    parts = lax.all_to_all(narrow, PAIRS, 0, 0)
    inverse, kept, sent = inverse_rows(
        jnp.stack([c, core]), ours, theirs, panel_ridge, panel, gathered
    )
    factor_part = (kept + lax.ppermute(sent, "core", SWAP)).astype(jnp.float16)
    factor_parts = lax.all_to_all(factor_part, PAIRS, 0, 0)
    row_ids = t * row_blk + jnp.arange(row_blk, dtype=jnp.int32)
    row_ridge = lax.dynamic_slice_in_dim(ridge, t * row_blk, row_blk)
    spread = jnp.where(row_ids[:, None] == panel_ids[None, :], row_ridge[:, None], 0.0)
    ridge_part = lax.dot_general(
        spread, inverse, NT, precision=HIGH, preferred_element_type=jnp.float32
    )

    col_ids = c * width + jnp.arange(width, dtype=jnp.int32)
    normals = jnp.sum(parts.astype(jnp.float32), axis=0) + jnp.where(
        row_ids[:, None] == col_ids[None, :], row_ridge[:, None], 0.0
    )
    normals, ridge_part = lax.optimization_barrier((normals, ridge_part))
    factor = jnp.sum(factor_parts.astype(jnp.float32), axis=0) + ridge_part
    return (normals, factor)


def solution(mesh):
    split = Mesh(mesh.devices.reshape(tuple(SPLIT.values())), tuple(SPLIT))
    in_specs = (P(TRACK, COLS), P(TRACK), P(TRACK), P(), P(), P())
    out_specs = (P(TRACK, COLS), P(TRACK, COLS))
    return jax.shard_map(body, mesh=split, in_specs=in_specs, out_specs=out_specs, check_vma=False)
```

```python
import jax
import jax.numpy as jnp
from jax import lax
from jax.experimental import pallas as pl
from jax.experimental.pallas import tpu as pltpu
from jax.sharding import Mesh
from jax.sharding import PartitionSpec as P

PANEL = 1024
NB = 128
HALF = 64
SUB = 8
BLOCKS = PANEL // NB
LIST = 9
SLICES = 5
NN = (((1,), (0,)), ((), ()))
NT = (((1,), (1,)), ((), ()))
HIGH = lax.Precision.HIGHEST
SPLIT = {"x": 4, "yl": 2, "core": 2, "yh": 2, "z": 4}
TRACK = ("x", "yl", "core")
COLS = ("yh", "z")
PAIRS = ("x", "yl")
CHIPS = ("x", "yl", "yh", "z")
SWAP = [(0, 1), (1, 0)]
VMEM = pl.BlockSpec(memory_space=pltpu.VMEM)
SMEM = pl.BlockSpec(memory_space=pltpu.SMEM)


def gather(x, axis):
    copies = jnp.broadcast_to(x[None], (lax.axis_size(axis),) + x.shape)
    return lax.all_to_all(copies, axis, 0, 0)


def filter_kernel(first_ref, halo_ref, local_ref, start_ref, table_ref, taps_ref, out_ref, ext_ref):
    halo_rows = halo_ref.shape[0]
    row_count, columns = local_ref.shape
    ext_ref[:halo_rows] = halo_ref[...]
    ext_ref[halo_rows : halo_rows + row_count] = local_ref[...]
    ext_ref[halo_rows + row_count :] = jnp.zeros_like(ext_ref[halo_rows + row_count :])
    span = 2 * NB
    taps = taps_ref[...]
    tables = taps.shape[0]
    lane = lax.broadcasted_iota(jnp.int32, (NB, span), 1)
    for b in range(row_count // NB):
        rows = slice(b * NB, (b + 1) * NB)
        choice = lax.broadcasted_iota(jnp.int32, (NB, tables), 1) == table_ref[rows, :]
        row_taps = jnp.dot(
            choice.astype(jnp.float32).astype(jnp.bfloat16), taps, preferred_element_type=jnp.float32
        )
        skewed = pltpu.roll(row_taps, 0, 1, stride=1, stride_axis=0)
        source = first_ref[0] + b * NB - halo_rows + lane
        coefs = jnp.where(source >= start_ref[rows, :], skewed, 0.0).astype(jnp.bfloat16)
        window = ext_ref[b * NB : b * NB + span, :]
        summed = jnp.dot(coefs, window, preferred_element_type=jnp.float32)
        turned = summed.T.astype(jnp.bfloat16)
        for copy in range(out_ref.shape[0]):
            out_ref[copy, :, rows] = turned


def filter_rows(local, ext_top, seg_start, seg_table, taps, first_row, copies):
    row_count, columns = local.shape
    flipped = jnp.pad(taps[:, ::-1], ((0, 0), (0, 2 * NB - taps.shape[1])))
    return pl.pallas_call(
        filter_kernel,
        out_shape=jax.ShapeDtypeStruct((copies, columns, row_count), jnp.bfloat16),
        in_specs=[SMEM] + [VMEM] * 5,
        out_specs=VMEM,
        scratch_shapes=[pltpu.VMEM((row_count + NB, columns), jnp.bfloat16)],
        compiler_params=pltpu.CompilerParams(vmem_limit_bytes=16 * 2**20),
    )(
        first_row.reshape(1),
        ext_top,
        local,
        seg_start[:, None],
        seg_table[:, None],
        flipped,
    )


def listed(c, h):
    own = (c < BLOCKS // 2) | (h < 2 * (BLOCKS - c))
    if isinstance(c, int):
        return (2 * c + h, c) if own else (7 + h, BLOCKS - 1 - c)
    return jnp.where(own, 2 * c + h, 7 + h), jnp.where(own, c, BLOCKS - 1 - c)


def panel_kernel(turn_ref, ids_ref, slab_ref, out_ref, panel_ref):
    cols, width, rows = slab_ref.shape
    part = 2 * NB
    lane = lax.broadcasted_iota(jnp.int32, (part, width), 1)
    for p in range(PANEL // part):
        ids = ids_ref[p * part : (p + 1) * part, :]
        acc = jnp.zeros((part, rows), jnp.float32)
        for k in range(cols):
            chosen = (lane == ids - k * width).astype(jnp.float32).astype(jnp.bfloat16)
            acc += jnp.dot(chosen, slab_ref[k], preferred_element_type=jnp.float32)
        panel_ref[p * part : (p + 1) * part, :] = acc.astype(jnp.bfloat16)
    turn = turn_ref[0]
    for h in range(LIST):
        i, j = listed(turn, h)
        left = panel_ref[pl.ds(pl.multiple_of(i * HALF, HALF), HALF), :]
        right = panel_ref[pl.ds(pl.multiple_of(j * NB, NB), NB), :]
        out_ref[h * HALF : (h + 1) * HALF, :] = lax.dot_general(
            left, right, NT, preferred_element_type=jnp.float32
        )
    out_ref[LIST * HALF :, :] = jnp.zeros_like(out_ref[LIST * HALF :, :])


def panel_parts(turn, panel_ids, slab, track):
    rows = slab.shape[-1]
    return pl.pallas_call(
        panel_kernel,
        out_shape=(
            jax.ShapeDtypeStruct((track * SLICES * SUB, NB), jnp.float32),
            jax.ShapeDtypeStruct((PANEL, rows), jnp.bfloat16),
        ),
        in_specs=[SMEM, VMEM, VMEM],
        out_specs=(VMEM, VMEM),
        compiler_params=pltpu.CompilerParams(vmem_limit_bytes=20 * 2**20),
    )(turn.reshape(1), panel_ids[:, None], slab)


def halves(a):
    high = a.astype(jnp.bfloat16)
    return high, (a - high.astype(jnp.float32)).astype(jnp.bfloat16)


def product(a, b, dims=NN):
    (ah, al), (bh, bl) = halves(a), halves(b)

    def dot(u, v):
        return lax.dot_general(u, v, dims, preferred_element_type=jnp.float32)

    return dot(ah, bh) + (dot(ah, bl) + dot(al, bh))


def reciprocal(x):
    guess = pl.reciprocal(x, approx=True)
    return guess * (2.0 - x * guess)


def factor_groups(groups, tasks):
    groups = list(groups)
    count = len(groups)
    shape = (SUB, NB)
    lane = lax.broadcasted_iota(jnp.int32, shape, 1)
    sub = lax.broadcasted_iota(jnp.int32, shape, 0)
    share = -(-len(tasks) // count)
    for s in range(count):
        top = groups[s]
        base = s * SUB
        more = s + 1 < count

        def column(g, j):
            return jnp.broadcast_to(groups[g][:, base + j : base + j + 1], shape)

        rows = [jnp.broadcast_to(top[i : i + 1, :], shape) for i in range(SUB)]
        t = {}
        for i in range(SUB):
            for j in range(i + 1):
                t[i, j] = jnp.broadcast_to(rows[i][:, base + j : base + j + 1], shape)
        inside = (lane >= base) & (lane < base + SUB)
        for i in range(SUB):
            rows[i] = jnp.where(inside, (lane == base + i).astype(jnp.float32), rows[i])
        r, u = [], {}
        if more:
            below = [column(s + 1, j) for j in range(SUB)]
            following = jnp.where(inside, 0.0, groups[s + 1])
        for k in range(0, SUB, 2):
            n = k + 1
            a, b = t[k, k], t[n, k]
            r.append(reciprocal(a))
            r.append(a * reciprocal(a * t[n, n] - b * b))
            for i in range(n, SUB):
                u[i, k] = t[i, k] * r[k]
            t[n, n] = t[n, n] - b * u[n, k]
            for i in range(n + 1, SUB):
                t[i, n] = t[i, n] - u[i, k] * b
                u[i, n] = t[i, n] * r[n]
            for j in range(n + 1, SUB):
                for i in range(j, SUB):
                    t[i, j] = (t[i, j] - u[i, k] * t[j, k]) - u[i, n] * t[j, n]
            for q in (k, n):
                for i in range(q + 1, SUB):
                    rows[i] = rows[i] - u[i, q] * rows[q]
                    if more:
                        below[i] = below[i] - u[i, q] * below[q]
                if more:
                    following = following - (below[q] * r[q]) * rows[q]
        scale = [lax.rsqrt(t[i, i]) for i in range(SUB)]
        packed = rows[0] * scale[0]
        for i in range(1, SUB):
            packed = jnp.where(sub == i, rows[i] * scale[i], packed)
        groups[s] = packed
        if more:
            groups[s + 1] = following
        if s + 2 < count:
            back = [None] * SUB
            for j in reversed(range(SUB)):
                acc = rows[j] * r[j]
                for i in range(j + 1, SUB):
                    acc = acc - u[i, j] * back[i]
                back[j] = acc
            for g in range(s + 2, count):
                acc = jnp.where(inside, 0.0, groups[g])
                for j in reversed(range(SUB)):
                    acc = acc - column(g, j) * back[j]
                groups[g] = acc
        for task in tasks[s * share : (s + 1) * share]:
            task()
    return groups


def block(i):
    return slice(i * NB, (i + 1) * NB)


def place_pieces(side, ours_ref, theirs_ref, ridge_ref, work_ref):
    chips = ours_ref.shape[0]
    cols = BLOCKS
    for place in range(chips):
        pair, c = divmod(place, cols)
        for core in range(2):
            t = 2 * pair + core
            for e in range(SLICES):
                h, row = divmod(SLICES * t + e, HALF // SUB)
                if h >= LIST:
                    continue
                i, j = listed(c, h)
                here = slice(e * SUB, (e + 1) * SUB)
                value = jnp.where(
                    side == core, ours_ref[place, here, :], theirs_ref[place, here, :]
                )
                first = i * HALF + row * SUB
                work_ref[first : first + SUB, block(j)] = value
    eye = lax.broadcasted_iota(jnp.int32, (NB, NB), 0) == lax.broadcasted_iota(
        jnp.int32, (NB, NB), 1
    )
    for m in range(BLOCKS):
        work_ref[block(m), block(m)] += jnp.where(eye, ridge_ref[:, block(m)], 0.0)


def inverse_kernel(
    place_ref,
    ours_ref,
    theirs_ref,
    ridge_ref,
    panel_ref,
    slab_ref,
    out_ref,
    kept_ref,
    sent_ref,
    work_ref,
):
    place_pieces(place_ref[1], ours_ref, theirs_ref, ridge_ref, work_ref)
    triangle = lax.broadcasted_iota(jnp.int32, (NB, NB), 0) >= lax.broadcasted_iota(
        jnp.int32, (NB, NB), 1
    )
    tasks = []
    for m in range(BLOCKS):
        groups = [
            work_ref[m * NB + SUB * g : m * NB + SUB * (g + 1), block(m)] for g in range(NB // SUB)
        ]
        groups = factor_groups(groups, tasks)
        inverse = jnp.where(triangle, jnp.concatenate(groups, axis=0), 0.0)
        tasks = []
        left = {}
        if m + 1 < BLOCKS:
            left[m + 1] = product(work_ref[block(m + 1), block(m)], inverse, NT)
            work_ref[block(m + 1), block(m + 1)] -= product(left[m + 1], left[m + 1], NT)

        def finish(m=m, inverse=inverse):
            if m:
                work_ref[block(m), : m * NB] = product(inverse, work_ref[block(m), : m * NB])
            work_ref[block(m), block(m)] = inverse

        def solve(i, m=m, inverse=inverse, left=left):
            left[i] = product(work_ref[block(i), block(m)], inverse, NT)

        def spread(i, m=m, left=left):
            if m:
                work_ref[block(i), : m * NB] -= product(left[i], work_ref[block(m), : m * NB])
            work_ref[block(i), block(m)] = -product(left[i], work_ref[block(m), block(m)])

        def update(i, j, left=left):
            work_ref[block(i), block(j)] -= product(left[i], left[j], NT)

        tasks.append(finish)
        for i in range(m + 1, BLOCKS):
            if i > m + 1:
                tasks.append(lambda i=i, solve=solve: solve(i))
            tasks.append(lambda i=i, spread=spread: spread(i))
            for j in range(m + 1, i + 1):
                if i > m + 1:
                    tasks.append(lambda i=i, j=j, update=update: update(i, j))
    for task in tasks:
        task()
    turn = place_ref[0]
    row = lax.broadcasted_iota(jnp.int32, out_ref.shape, 0) + turn * NB
    col = lax.broadcasted_iota(jnp.int32, out_ref.shape, 1)
    mine = work_ref[pl.ds(pl.multiple_of(turn * NB, NB), NB), :]
    mine = jnp.where(row >= col, mine, 0.0)
    out_ref[...] = mine
    panel = panel_ref[...]
    whitened = sum(jnp.dot(x, panel, preferred_element_type=jnp.float32) for x in halves(mine))
    both = jnp.concatenate(halves(whitened), axis=0)
    count, row_blk, _ = kept_ref.shape
    for side, part_ref in ((place_ref[1], kept_ref), (1 - place_ref[1], sent_ref)):
        for k in range(count):
            rows = slab_ref[k, pl.ds(pl.multiple_of(side * row_blk, row_blk), row_blk), :]
            twice = lax.dot_general(rows, both, NT, preferred_element_type=jnp.float32)
            part_ref[k] = twice[:, :NB] + twice[:, NB:]


def inverse_rows(place, ours, theirs, panel_ridge, panel, slab):
    count, width, _ = slab.shape
    part = jax.ShapeDtypeStruct((count, width // 2, NB), jnp.float32)
    return pl.pallas_call(
        inverse_kernel,
        out_shape=(
            jax.ShapeDtypeStruct((NB, PANEL), jnp.float32),
            part,
            part,
        ),
        in_specs=[SMEM] + [VMEM] * 5,
        out_specs=(VMEM, VMEM, VMEM),
        scratch_shapes=[pltpu.VMEM((PANEL, PANEL), jnp.float32)],
        cost_estimate=pl.CostEstimate(
            flops=38 * 10**9, transcendentals=4 * PANEL, bytes_accessed=12 * 2**20
        ),
        compiler_params=pltpu.CompilerParams(vmem_limit_bytes=24 * 2**20),
    )(place, ours, theirs, panel_ridge[None, :], panel, slab)


def body(design, seg_start, seg_table, taps, ridge, col_perm):
    row_count, width = design.shape
    halo_rows = taps.shape[1] - 1
    track, cols = lax.axis_size(TRACK), lax.axis_size(COLS)
    t, c, core = lax.axis_index(TRACK), lax.axis_index(COLS), lax.axis_index("core")
    slab = width * cols
    row_blk = slab // track
    panel_ids = col_perm[:PANEL]

    pairs = [(i, i + 1) for i in range(track - 1)]
    ext_top = lax.ppermute(design[row_count - halo_rows :], TRACK, pairs)
    copies = filter_rows(design, ext_top, seg_start, seg_table, taps, t * row_count, cols)
    gathered = lax.all_to_all(copies, COLS, 0, 0)
    filtered = copies[0]

    block_part, panel = panel_parts(c, panel_ids, gathered, track)
    slab_rows, block_part = lax.optimization_barrier((gathered, block_part))
    slab_rows = slab_rows.reshape(track // 2, 2, row_blk, row_count)
    block_parts = lax.all_to_all(block_part.reshape(track, SLICES * SUB, NB), TRACK, 0, 0)

    def rows_of(side):
        rows = lax.dynamic_index_in_dim(slab_rows, side, 1, keepdims=False)
        return lax.dot_general(
            rows, filtered, (((2,), (1,)), ((), ())), preferred_element_type=jnp.float32
        )

    sent, block_sum = lax.optimization_barrier((rows_of(1 - core), jnp.sum(block_parts, axis=0)))
    ours = gather(block_sum, CHIPS)
    late_ids, _ = lax.optimization_barrier((panel_ids, block_sum))
    panel_ridge = jnp.take(ridge, late_ids)
    sums = rows_of(core) + lax.ppermute(sent, "core", SWAP)
    narrow, ours, panel_ridge = lax.optimization_barrier(
        (sums.astype(jnp.float16), ours, panel_ridge)
    )
    theirs = lax.ppermute(ours, "core", SWAP)
    parts = lax.all_to_all(narrow, PAIRS, 0, 0)
    inverse, kept, sent = inverse_rows(
        jnp.stack([c, core]), ours, theirs, panel_ridge, panel, gathered
    )
    factor_part = (kept + lax.ppermute(sent, "core", SWAP)).astype(jnp.float16)
    factor_parts = lax.all_to_all(factor_part, PAIRS, 0, 0)
    row_ids = t * row_blk + jnp.arange(row_blk, dtype=jnp.int32)
    row_ridge = lax.dynamic_slice_in_dim(ridge, t * row_blk, row_blk)
    spread = jnp.where(row_ids[:, None] == panel_ids[None, :], row_ridge[:, None], 0.0)
    ridge_part = lax.dot_general(
        spread, inverse, NT, precision=HIGH, preferred_element_type=jnp.float32
    )

    col_ids = c * width + jnp.arange(width, dtype=jnp.int32)
    normals = jnp.sum(parts.astype(jnp.float32), axis=0) + jnp.where(
        row_ids[:, None] == col_ids[None, :], row_ridge[:, None], 0.0
    )
    normals, ridge_part = lax.optimization_barrier((normals, ridge_part))
    factor = jnp.sum(factor_parts.astype(jnp.float32), axis=0) + ridge_part
    return (normals, factor)


def solution(mesh):
    split = Mesh(mesh.devices.reshape(tuple(SPLIT.values())), tuple(SPLIT))
    in_specs = (P(TRACK, COLS), P(TRACK), P(TRACK), P(), P(), P())
    out_specs = (P(TRACK, COLS), P(TRACK, COLS))
    return jax.shard_map(body, mesh=split, in_specs=in_specs, out_specs=out_specs, check_vma=False)
```

```python
import jax
import jax.numpy as jnp
from jax import lax
from jax.experimental import pallas as pl
from jax.experimental.pallas import tpu as pltpu
from jax.sharding import Mesh
from jax.sharding import PartitionSpec as P

PANEL = 1024
NB = 128
HALF = 64
SUB = 8
BLOCKS = PANEL // NB
LIST = 9
SLICES = 5
NN = (((1,), (0,)), ((), ()))
NT = (((1,), (1,)), ((), ()))
HIGH = lax.Precision.HIGHEST
SPLIT = {"x": 4, "yl": 2, "core": 2, "yh": 2, "z": 4}
TRACK = ("x", "yl", "core")
COLS = ("yh", "z")
PAIRS = ("x", "yl")
CHIPS = ("x", "yl", "yh", "z")
SWAP = [(0, 1), (1, 0)]
VMEM = pl.BlockSpec(memory_space=pltpu.VMEM)
SMEM = pl.BlockSpec(memory_space=pltpu.SMEM)


def gather(x, axis):
    copies = jnp.broadcast_to(x[None], (lax.axis_size(axis),) + x.shape)
    return lax.all_to_all(copies, axis, 0, 0)


def filter_kernel(first_ref, halo_ref, local_ref, marks_ref, taps_ref, out_ref, ext_ref):
    halo_rows = halo_ref.shape[0]
    row_count, columns = local_ref.shape
    ext_ref[:halo_rows] = halo_ref[...]
    ext_ref[halo_rows : halo_rows + row_count] = local_ref[...]
    ext_ref[halo_rows + row_count :] = jnp.zeros_like(ext_ref[halo_rows + row_count :])
    span = 2 * NB
    taps = taps_ref[...]
    tables = taps.shape[0]
    lane = lax.broadcasted_iota(jnp.int32, (NB, span), 1)
    for b in range(row_count // NB):
        rows = slice(b * NB, (b + 1) * NB)
        choice = lax.broadcasted_iota(jnp.int32, (NB, tables), 1) == marks_ref[rows, 1:2]
        row_taps = jnp.dot(
            choice.astype(jnp.float32).astype(jnp.bfloat16), taps, preferred_element_type=jnp.float32
        )
        skewed = pltpu.roll(row_taps, 0, 1, stride=1, stride_axis=0)
        source = first_ref[0] + b * NB - halo_rows + lane
        coefs = jnp.where(source >= marks_ref[rows, 0:1], skewed, 0.0).astype(jnp.bfloat16)
        window = ext_ref[b * NB : b * NB + span, :]
        summed = jnp.dot(coefs, window, preferred_element_type=jnp.float32)
        turned = summed.T.astype(jnp.bfloat16)
        for copy in range(out_ref.shape[0]):
            out_ref[copy, :, rows] = turned


def filter_rows(local, ext_top, seg_start, seg_table, taps, first_row, copies):
    row_count, columns = local.shape
    flipped = jnp.pad(taps[:, ::-1], ((0, 0), (0, 2 * NB - taps.shape[1])))
    return pl.pallas_call(
        filter_kernel,
        out_shape=jax.ShapeDtypeStruct((copies, columns, row_count), jnp.bfloat16),
        in_specs=[SMEM] + [VMEM] * 4,
        out_specs=VMEM,
        scratch_shapes=[pltpu.VMEM((row_count + NB, columns), jnp.bfloat16)],
        compiler_params=pltpu.CompilerParams(vmem_limit_bytes=16 * 2**20),
    )(
        first_row.reshape(1),
        ext_top,
        local,
        jnp.stack([seg_start, seg_table], axis=1),
        flipped,
    )


def listed(c, h):
    own = (c < BLOCKS // 2) | (h < 2 * (BLOCKS - c))
    if isinstance(c, int):
        return (2 * c + h, c) if own else (7 + h, BLOCKS - 1 - c)
    return jnp.where(own, 2 * c + h, 7 + h), jnp.where(own, c, BLOCKS - 1 - c)


def panel_kernel(turn_ref, ids_ref, slab_ref, out_ref, panel_ref):
    cols, width, rows = slab_ref.shape
    part = 2 * NB
    lane = lax.broadcasted_iota(jnp.int32, (part, width), 1)
    for p in range(PANEL // part):
        ids = ids_ref[p * part : (p + 1) * part, :]
        acc = jnp.zeros((part, rows), jnp.float32)
        for k in range(cols):
            chosen = (lane == ids - k * width).astype(jnp.float32).astype(jnp.bfloat16)
            acc += jnp.dot(chosen, slab_ref[k], preferred_element_type=jnp.float32)
        panel_ref[p * part : (p + 1) * part, :] = acc.astype(jnp.bfloat16)
    turn = turn_ref[0]
    for h in range(LIST):
        i, j = listed(turn, h)
        left = panel_ref[pl.ds(pl.multiple_of(i * HALF, HALF), HALF), :]
        right = panel_ref[pl.ds(pl.multiple_of(j * NB, NB), NB), :]
        out_ref[h * HALF : (h + 1) * HALF, :] = lax.dot_general(
            left, right, NT, preferred_element_type=jnp.float32
        )
    out_ref[LIST * HALF :, :] = jnp.zeros_like(out_ref[LIST * HALF :, :])


def panel_parts(turn, panel_ids, slab, track):
    rows = slab.shape[-1]
    return pl.pallas_call(
        panel_kernel,
        out_shape=(
            jax.ShapeDtypeStruct((track * SLICES * SUB, NB), jnp.float32),
            jax.ShapeDtypeStruct((PANEL, rows), jnp.bfloat16),
        ),
        in_specs=[SMEM, VMEM, VMEM],
        out_specs=(VMEM, VMEM),
        compiler_params=pltpu.CompilerParams(vmem_limit_bytes=20 * 2**20),
    )(turn.reshape(1), panel_ids[:, None], slab)


def halves(a):
    high = a.astype(jnp.bfloat16)
    return high, (a - high.astype(jnp.float32)).astype(jnp.bfloat16)


def product(a, b, dims=NN):
    (ah, al), (bh, bl) = halves(a), halves(b)

    def dot(u, v):
        return lax.dot_general(u, v, dims, preferred_element_type=jnp.float32)

    return dot(ah, bh) + (dot(ah, bl) + dot(al, bh))


def reciprocal(x):
    guess = pl.reciprocal(x, approx=True)
    return guess * (2.0 - x * guess)


def factor_groups(groups, tasks):
    groups = list(groups)
    count = len(groups)
    shape = (SUB, NB)
    lane = lax.broadcasted_iota(jnp.int32, shape, 1)
    sub = lax.broadcasted_iota(jnp.int32, shape, 0)
    share = -(-len(tasks) // count)
    for s in range(count):
        top = groups[s]
        base = s * SUB
        more = s + 1 < count

        def column(g, j):
            return jnp.broadcast_to(groups[g][:, base + j : base + j + 1], shape)

        rows = [jnp.broadcast_to(top[i : i + 1, :], shape) for i in range(SUB)]
        t = {}
        for i in range(SUB):
            for j in range(i + 1):
                t[i, j] = jnp.broadcast_to(rows[i][:, base + j : base + j + 1], shape)
        inside = (lane >= base) & (lane < base + SUB)
        for i in range(SUB):
            rows[i] = jnp.where(inside, (lane == base + i).astype(jnp.float32), rows[i])
        r, u = [], {}
        if more:
            below = [column(s + 1, j) for j in range(SUB)]
            following = jnp.where(inside, 0.0, groups[s + 1])
        for k in range(0, SUB, 2):
            n = k + 1
            a, b = t[k, k], t[n, k]
            r.append(reciprocal(a))
            r.append(a * reciprocal(a * t[n, n] - b * b))
            for i in range(n, SUB):
                u[i, k] = t[i, k] * r[k]
            t[n, n] = t[n, n] - b * u[n, k]
            for i in range(n + 1, SUB):
                t[i, n] = t[i, n] - u[i, k] * b
                u[i, n] = t[i, n] * r[n]
            for j in range(n + 1, SUB):
                for i in range(j, SUB):
                    t[i, j] = (t[i, j] - u[i, k] * t[j, k]) - u[i, n] * t[j, n]
            for q in (k, n):
                for i in range(q + 1, SUB):
                    rows[i] = rows[i] - u[i, q] * rows[q]
                    if more:
                        below[i] = below[i] - u[i, q] * below[q]
                if more:
                    following = following - (below[q] * r[q]) * rows[q]
        scale = [lax.rsqrt(t[i, i]) for i in range(SUB)]
        packed = rows[0] * scale[0]
        for i in range(1, SUB):
            packed = jnp.where(sub == i, rows[i] * scale[i], packed)
        groups[s] = packed
        if more:
            groups[s + 1] = following
        if s + 2 < count:
            back = [None] * SUB
            for j in reversed(range(SUB)):
                acc = rows[j] * r[j]
                for i in range(j + 1, SUB):
                    acc = acc - u[i, j] * back[i]
                back[j] = acc
            for g in range(s + 2, count):
                acc = jnp.where(inside, 0.0, groups[g])
                for j in reversed(range(SUB)):
                    acc = acc - column(g, j) * back[j]
                groups[g] = acc
        for task in tasks[s * share : (s + 1) * share]:
            task()
    return groups


def block(i):
    return slice(i * NB, (i + 1) * NB)


def place_pieces(side, ours_ref, theirs_ref, ridge_ref, work_ref):
    chips = ours_ref.shape[0]
    cols = BLOCKS
    for place in range(chips):
        pair, c = divmod(place, cols)
        for core in range(2):
            t = 2 * pair + core
            for e in range(SLICES):
                h, row = divmod(SLICES * t + e, HALF // SUB)
                if h >= LIST:
                    continue
                i, j = listed(c, h)
                here = slice(e * SUB, (e + 1) * SUB)
                value = jnp.where(
                    side == core, ours_ref[place, here, :], theirs_ref[place, here, :]
                )
                first = i * HALF + row * SUB
                work_ref[first : first + SUB, block(j)] = value
    eye = lax.broadcasted_iota(jnp.int32, (NB, NB), 0) == lax.broadcasted_iota(
        jnp.int32, (NB, NB), 1
    )
    for m in range(BLOCKS):
        work_ref[block(m), block(m)] += jnp.where(eye, ridge_ref[:, block(m)], 0.0)


def inverse_kernel(
    place_ref,
    ours_ref,
    theirs_ref,
    ridge_ref,
    panel_ref,
    slab_ref,
    out_ref,
    kept_ref,
    sent_ref,
    work_ref,
):
    place_pieces(place_ref[1], ours_ref, theirs_ref, ridge_ref, work_ref)
    triangle = lax.broadcasted_iota(jnp.int32, (NB, NB), 0) >= lax.broadcasted_iota(
        jnp.int32, (NB, NB), 1
    )
    tasks = []
    for m in range(BLOCKS):
        groups = [
            work_ref[m * NB + SUB * g : m * NB + SUB * (g + 1), block(m)] for g in range(NB // SUB)
        ]
        groups = factor_groups(groups, tasks)
        inverse = jnp.where(triangle, jnp.concatenate(groups, axis=0), 0.0)
        tasks = []
        left = {}
        if m + 1 < BLOCKS:
            left[m + 1] = product(work_ref[block(m + 1), block(m)], inverse, NT)
            work_ref[block(m + 1), block(m + 1)] -= product(left[m + 1], left[m + 1], NT)

        def finish(m=m, inverse=inverse):
            if m:
                work_ref[block(m), : m * NB] = product(inverse, work_ref[block(m), : m * NB])
            work_ref[block(m), block(m)] = inverse

        def solve(i, m=m, inverse=inverse, left=left):
            left[i] = product(work_ref[block(i), block(m)], inverse, NT)

        def spread(i, m=m, left=left):
            if m:
                work_ref[block(i), : m * NB] -= product(left[i], work_ref[block(m), : m * NB])
            work_ref[block(i), block(m)] = -product(left[i], work_ref[block(m), block(m)])

        def update(i, j, left=left):
            work_ref[block(i), block(j)] -= product(left[i], left[j], NT)

        tasks.append(finish)
        for i in range(m + 1, BLOCKS):
            if i > m + 1:
                tasks.append(lambda i=i, solve=solve: solve(i))
            tasks.append(lambda i=i, spread=spread: spread(i))
            for j in range(m + 1, i + 1):
                if i > m + 1:
                    tasks.append(lambda i=i, j=j, update=update: update(i, j))
    for task in tasks:
        task()
    turn = place_ref[0]
    row = lax.broadcasted_iota(jnp.int32, out_ref.shape, 0) + turn * NB
    col = lax.broadcasted_iota(jnp.int32, out_ref.shape, 1)
    mine = work_ref[pl.ds(pl.multiple_of(turn * NB, NB), NB), :]
    mine = jnp.where(row >= col, mine, 0.0)
    out_ref[...] = mine
    panel = panel_ref[...]
    whitened = sum(jnp.dot(x, panel, preferred_element_type=jnp.float32) for x in halves(mine))
    both = jnp.concatenate(halves(whitened), axis=0)
    count, row_blk, _ = kept_ref.shape
    for side, part_ref in ((place_ref[1], kept_ref), (1 - place_ref[1], sent_ref)):
        for k in range(count):
            rows = slab_ref[k, pl.ds(pl.multiple_of(side * row_blk, row_blk), row_blk), :]
            twice = lax.dot_general(rows, both, NT, preferred_element_type=jnp.float32)
            part_ref[k] = twice[:, :NB] + twice[:, NB:]


def inverse_rows(place, ours, theirs, panel_ridge, panel, slab):
    count, width, _ = slab.shape
    part = jax.ShapeDtypeStruct((count, width // 2, NB), jnp.float32)
    return pl.pallas_call(
        inverse_kernel,
        out_shape=(
            jax.ShapeDtypeStruct((NB, PANEL), jnp.float32),
            part,
            part,
        ),
        in_specs=[SMEM] + [VMEM] * 5,
        out_specs=(VMEM, VMEM, VMEM),
        scratch_shapes=[pltpu.VMEM((PANEL, PANEL), jnp.float32)],
        cost_estimate=pl.CostEstimate(
            flops=38 * 10**9, transcendentals=4 * PANEL, bytes_accessed=12 * 2**20
        ),
        compiler_params=pltpu.CompilerParams(vmem_limit_bytes=24 * 2**20),
    )(place, ours, theirs, panel_ridge[None, :], panel, slab)


def body(design, seg_start, seg_table, taps, ridge, col_perm):
    row_count, width = design.shape
    halo_rows = taps.shape[1] - 1
    track, cols = lax.axis_size(TRACK), lax.axis_size(COLS)
    t, c, core = lax.axis_index(TRACK), lax.axis_index(COLS), lax.axis_index("core")
    slab = width * cols
    row_blk = slab // track
    panel_ids = col_perm[:PANEL]

    pairs = [(i, i + 1) for i in range(track - 1)]
    ext_top = lax.ppermute(design[row_count - halo_rows :], TRACK, pairs)
    copies = filter_rows(design, ext_top, seg_start, seg_table, taps, t * row_count, cols)
    gathered = lax.all_to_all(copies, COLS, 0, 0)
    filtered = copies[0]

    block_part, panel = panel_parts(c, panel_ids, gathered, track)
    slab_rows, block_part = lax.optimization_barrier((gathered, block_part))
    slab_rows = slab_rows.reshape(track // 2, 2, row_blk, row_count)
    block_parts = lax.all_to_all(block_part.reshape(track, SLICES * SUB, NB), TRACK, 0, 0)

    def rows_of(side):
        rows = lax.dynamic_index_in_dim(slab_rows, side, 1, keepdims=False)
        return lax.dot_general(
            rows, filtered, (((2,), (1,)), ((), ())), preferred_element_type=jnp.float32
        )

    sent, block_sum = lax.optimization_barrier((rows_of(1 - core), jnp.sum(block_parts, axis=0)))
    ours = gather(block_sum, CHIPS)
    late_ids, _ = lax.optimization_barrier((panel_ids, block_sum))
    panel_ridge = jnp.take(ridge, late_ids)
    sums = rows_of(core) + lax.ppermute(sent, "core", SWAP)
    narrow, ours, panel_ridge = lax.optimization_barrier(
        (sums.astype(jnp.float16), ours, panel_ridge)
    )
    theirs = lax.ppermute(ours, "core", SWAP)
    parts = lax.all_to_all(narrow, PAIRS, 0, 0)
    inverse, kept, sent = inverse_rows(
        jnp.stack([c, core]), ours, theirs, panel_ridge, panel, gathered
    )
    factor_part = (kept + lax.ppermute(sent, "core", SWAP)).astype(jnp.float16)
    factor_parts = lax.all_to_all(factor_part, PAIRS, 0, 0)
    row_ids = t * row_blk + jnp.arange(row_blk, dtype=jnp.int32)
    row_ridge = lax.dynamic_slice_in_dim(ridge, t * row_blk, row_blk)
    spread = jnp.where(row_ids[:, None] == panel_ids[None, :], row_ridge[:, None], 0.0)
    ridge_part = lax.dot_general(
        spread, inverse, NT, precision=HIGH, preferred_element_type=jnp.float32
    )

    col_ids = c * width + jnp.arange(width, dtype=jnp.int32)
    normals = jnp.sum(parts.astype(jnp.float32), axis=0) + jnp.where(
        row_ids[:, None] == col_ids[None, :], row_ridge[:, None], 0.0
    )
    normals, ridge_part = lax.optimization_barrier((normals, ridge_part))
    factor = jnp.sum(factor_parts.astype(jnp.float32), axis=0) + ridge_part
    return (normals, factor)


def solution(mesh):
    split = Mesh(mesh.devices.reshape(tuple(SPLIT.values())), tuple(SPLIT))
    in_specs = (P(TRACK, COLS), P(TRACK), P(TRACK), P(), P(), P())
    out_specs = (P(TRACK, COLS), P(TRACK, COLS))
    return jax.shard_map(body, mesh=split, in_specs=in_specs, out_specs=out_specs, check_vma=False)
```
